256 devices in a mesh: store: 16 (over x, y), head: 16 (over z, core).
Axes of the slice: x: 4, y: 4, z: 8, core: 2. Of those that a mesh axis runs over, the one named last changes fastest.
Arguments:
- queries: bfloat16 [64, 1024, 4096], P('store', None, 'head'), may hold values from -64 to 64
- kv_store: bfloat16 [128, 2, 64, 4096], P('store', None, None, 'head'), may hold values from -6 to 6
- hidden_rows: bfloat16 [64, 128, 8192], P('store', None, 'head'), may hold values from -6 to 6
- w_kv: bfloat16 [8192, 2, 4096], P('store', None, 'head'), may hold values from -0.0625 to 0.0625
- passage_ids: int32 [64, 16], replicated, may hold values from 0 to 127, as said below
- passage_home: int32 [128], replicated, may hold values from 0 to 127, as said below
- passage_counts: int32 [64], replicated, may hold values from 8 to 16, as said below
- recompute_pos: int32 [64, 128], P('store'), may hold values from 0 to 1023, as said below
Outputs:
- attended: bfloat16 [64, 1024, 4096], P('store', None, 'head')
The draws below stay inside these ranges and needn't reach their ends.
Inputs may be any that keep to these rules, and one draw needn't show every extreme that they name: passage_home: a permutation; passage p lies in row passage_home[p] of kv_store, on store device passage_home[p] // 8. passage_ids: the 16 passages of one request are distinct, and every store device holds exactly 1 of them; slots at or past passage_counts are named but not used. passage_counts: some request uses all 16 slots. recompute_pos: the 128 positions of one request are distinct and lie below passage_counts times 64.
All inputs are finite; a program needn't handle non-finite values.
Results may differ from the reference program's by a relative error of at most 0.0054.
Values may be sent and summed in bfloat16 or wider, within the bound.
A program may use at most 128 MiB of HBM per device.

```python
import jax
import jax.numpy as jnp
from jax import lax

D = 8192
HD = 128
H = 32
QLEN = 1024
SEL = 128
BLK = 64
MAXP = 16
PASS_DEV = 8
REQUESTS = 64
PASSAGES = 128
N_STORE = 16


def placement_tables(key):
    home_rows = jax.random.permutation(jax.random.fold_in(key, 11), PASSAGES).astype(jnp.int32)
    inverse = jnp.argsort(home_rows).astype(jnp.int32)
    order_keys = jax.random.split(jax.random.fold_in(key, 12), REQUESTS)
    device_order = jax.vmap(lambda single: jax.random.permutation(single, N_STORE))(order_keys).astype(jnp.int32)
    row_offset = jax.random.randint(jax.random.fold_in(key, 13), (REQUESTS, N_STORE), 0, PASS_DEV).astype(jnp.int32)
    slot_index = jnp.arange(MAXP, dtype=jnp.int32)
    slot_level = slot_index // N_STORE
    chosen_dev = device_order[:, slot_index % N_STORE]
    local_row = (row_offset[:, slot_index % N_STORE] + slot_level[None, :]) % PASS_DEV
    store_row = chosen_dev * PASS_DEV + local_row
    return (home_rows, inverse[store_row].astype(jnp.int32))


def request_lengths(key):
    lengths = jax.random.randint(jax.random.fold_in(key, 21), (REQUESTS,), MAXP // 2, MAXP + 1).astype(jnp.int32)
    full_request = jax.random.randint(jax.random.fold_in(key, 22), (), 0, REQUESTS)
    return lengths.at[full_request].set(MAXP).astype(jnp.int32)


def draw_passage_home(key, part):
    return placement_tables(key)[0]


def draw_passage_ids(key, part):
    return placement_tables(key)[1]


def draw_passage_counts(key, part):
    return request_lengths(key)


def draw_recompute_pos(key, part):
    lengths = request_lengths(key)
    key = jax.random.fold_in(key, 31)
    span = MAXP * BLK
    request_keys = jax.random.split(key, REQUESTS)
    shuffled = jax.vmap(lambda single: jax.random.permutation(single, span))(request_keys).astype(jnp.int32)
    position = jnp.arange(span, dtype=jnp.int32)
    ranking = shuffled + jnp.where(position[None, :] >= lengths[:, None] * BLK, span, 0).astype(jnp.int32)
    order = jnp.argsort(ranking, axis=1, stable=True).astype(jnp.int32)
    return order[:, :SEL]


def draw_queries(key, part):
    key = jax.random.fold_in(key, 7)
    full_shape = (REQUESTS, QLEN, H * HD)
    values = jnp.clip(jax.random.normal(key, full_shape, jnp.float32), -6.0, 6.0)
    return values.astype(jnp.bfloat16)


def block_levels(stream_key, shape, cuts, least, top_value):
    loudness = 1.0
    for dim, shards_of in cuts:
        steps = jax.random.uniform(jax.random.fold_in(jax.random.fold_in(stream_key, 6), dim), (shards_of,), jnp.float32, least / len(cuts), top_value / len(cuts))
        loudness = loudness * jnp.repeat(jnp.exp(steps), shape[dim] // shards_of).reshape((-1,) + (1,) * (len(shape) - 1 - dim))
    return loudness


def normal_values(stream_key, extent, spread, reach, cuts=(), held_as=jnp.bfloat16):
    drawn = spread * jax.random.normal(stream_key, extent, jnp.float32)
    if cuts:
        drawn = drawn * block_levels(stream_key, extent, cuts, -0.22, 0.18)
    return jnp.clip(drawn, -reach, reach).astype(held_as)


def setup_inputs(seed: int = 0) -> dict:
    keys = jax.random.split(jax.random.key(seed), 9)
    return {
        "queries": draw_queries(jax.random.fold_in(keys[8], 71), 0),
        "kv_store": normal_values(keys[1], (PASSAGES, 2, BLK, H * HD), 1.0, 6.0, ((0, 16), (3, 16))),
        "hidden_rows": normal_values(keys[2], (REQUESTS, SEL, D), 1.0, 6.0, ((0, 16), (2, 16))),
        "w_kv": normal_values(keys[3], (D, 2, H * HD), D ** -0.5, 0.0625, ((0, 16), (2, 16))),
        "passage_ids": draw_passage_ids(jax.random.fold_in(keys[8], 71), 0),
        "passage_home": draw_passage_home(jax.random.fold_in(keys[8], 71), 0),
        "passage_counts": draw_passage_counts(jax.random.fold_in(keys[8], 71), 0),
        "recompute_pos": draw_recompute_pos(jax.random.fold_in(keys[8], 71), 0),
    }


EPS = 1e-06

def normalize(hidden):
    widened = hidden.astype(jnp.float32)
    inv_rms = lax.rsqrt(lax.optimization_barrier(jnp.mean(widened * widened, axis=-1, keepdims=True)) + EPS)
    return (widened * inv_rms).astype(jnp.bfloat16)

def attend(query_rows, context, positions, recomputed, used_slots):
    slot_count, _, block_len, feat_width = context.shape
    key_rows = context[:, 0].reshape(slot_count * block_len, feat_width)
    value_rows = context[:, 1].reshape(slot_count * block_len, feat_width)
    key_rows = key_rows.at[positions].set(recomputed[:, :feat_width])
    value_rows = value_rows.at[positions].set(recomputed[:, feat_width:])
    head_count = feat_width // HD
    query_heads = query_rows.reshape(query_rows.shape[0], head_count, HD)
    key_heads = key_rows.reshape(-1, head_count, HD)
    value_heads = value_rows.reshape(-1, head_count, HD)
    scores = jnp.einsum('qhd,khd->hqk', query_heads.astype(jnp.float32), key_heads.astype(jnp.float32)) * HD ** (-0.5)
    usable = jnp.arange(slot_count * block_len) < used_slots * block_len
    scores = jnp.where(usable[None, None, :], scores, -jnp.inf)
    largest = lax.optimization_barrier(jnp.max(scores, axis=-1, keepdims=True))
    exps = jnp.exp(scores - largest)
    attn_weights = (exps / lax.optimization_barrier(jnp.sum(exps, axis=-1, keepdims=True))).astype(jnp.bfloat16)
    mixed = jnp.einsum('hqk,khd->qhd', attn_weights.astype(jnp.float32), value_heads.astype(jnp.float32))
    return mixed.reshape(query_rows.shape[0], feat_width).astype(jnp.bfloat16)

def reference(queries, kv_store, hidden_rows, w_kv, passage_ids, passage_home, passage_counts, recompute_pos):
    normed = normalize(hidden_rows.reshape(REQUESTS * SEL, D))
    projection = w_kv.reshape(D, 2 * H * HD)
    recomputed = jnp.dot(normed, projection, preferred_element_type=jnp.float32).astype(jnp.bfloat16)
    recomputed = recomputed.reshape(REQUESTS, SEL, 2 * H * HD)

    def one_request(inputs):
        query_rows, id_row, used_slots, positions, new_rows = inputs
        context = kv_store[passage_home[id_row]]
        return attend(query_rows, context, positions, new_rows, used_slots)
    return lax.map(one_request, (queries, passage_ids, passage_counts, recompute_pos, recomputed))
```

```python
import math

import jax
import jax.numpy as jnp
from jax import lax
from jax.experimental import pallas as pl
from jax.experimental.pallas import tpu as pltpu
from jax.sharding import PartitionSpec as P

MESH = pl.DeviceIdType.MESH

D = 8192
HD = 128
EPS = 1e-06
SLOTS = 16
BLK = 64
SPAN = SLOTS * BLK
REQS = 4
QLEN = 1024
SEL = 128
FEAT = 256
ROWS = REQS * SEL
DEEP = 512
QTILE = 256
MASKED = -1e30
TO_BASE_TWO = HD ** (-0.5) * math.log2(math.e)

NT = (((1,), (1,)), ((), ()))
NN = (((1,), (0,)), ((), ()))


def dot(a, b, dims):
    return lax.dot_general(a, b, dims, preferred_element_type=jnp.float32)


def remote(src, dst, send_sem, recv_sem, device):
    return pltpu.make_async_remote_copy(
        src_ref=src,
        dst_ref=dst,
        send_sem=send_sem,
        recv_sem=recv_sem,
        device_id=device,
        device_id_type=MESH,
    )


class Ring4:
    def __init__(self, at, me, plus, minus, send, recv):
        self.at, self.plus, self.minus, self.send, self.recv = at, plus, minus, send, recv
        self.me, self.prev, self.next, self.far = me, (me + 3) % 4, (me + 1) % 4, (me + 2) % 4

    def copy(self, source, part, k, device):
        piece = self.at(source, part)
        return remote(piece, piece, self.send(k), self.recv(k), device)

    def start(self):
        self.copy(self.me, None, 0, self.plus).start()
        self.copy(self.me, None, 1, self.minus).start()

    def forward(self):
        self.copy(self.prev, None, 0, self.plus).wait_recv()
        self.copy(self.prev, 0, 2, self.plus).start()
        self.copy(self.next, None, 1, self.minus).wait_recv()
        self.copy(self.next, 1, 3, self.minus).start()

    def finish(self):
        self.copy(self.far, 0, 2, self.plus).wait_recv()
        self.copy(self.far, 1, 3, self.minus).wait_recv()

    def drain(self):
        self.copy(self.me, None, 0, self.plus).wait_send()
        self.copy(self.me, None, 1, self.minus).wait_send()
        self.copy(self.prev, 0, 2, self.plus).wait_send()
        self.copy(self.next, 1, 3, self.minus).wait_send()


def kernel(
    q_hbm, kv_hbm, x_hbm, w_hbm, table, bias, out_hbm,
    q, x_all, w_all, k_near, v_near, k_send, v_send, k_all, v_all,
    mixed, top, total, projected, squares, fresh, result,
    local_sem, out_sem, kv1_send, kv1_recv, kv2_send, kv2_recv,
    w1_send, w1_recv, w2_send, w2_recv, x_send, x_recv, pair_send, pair_recv,
):
    store, head = lax.axis_index("store"), lax.axis_index("head")
    x, y, z, core = store // 4, store % 4, head // 2, head % 2

    def at_xy(dx, dy):
        return {"store": ((x + dx) % 4) * 4 + (y + dy) % 4, "head": head}

    def at_z(dz):
        return {"store": store, "head": ((z + dz) % 8) * 2 + core}

    sibling = {"store": store, "head": z * 2 + (1 - core)}

    loads = [
        pltpu.make_async_copy(kv_hbm.at[:, 0], k_near.at[x], local_sem.at[0]),
        pltpu.make_async_copy(kv_hbm.at[:, 1], v_near.at[y], local_sem.at[1]),
        pltpu.make_async_copy(x_hbm, x_all.at[head], local_sem.at[2]),
        pltpu.make_async_copy(w_hbm, w_all.at[store], local_sem.at[3]),
        pltpu.make_async_copy(q_hbm, q, local_sem.at[4]),
    ]
    for load in loads:
        load.start()

    barrier = pltpu.get_barrier_semaphore()
    peers = [at_xy(d, 0) for d in (1, 3, 2)] + [at_xy(0, d) for d in (1, 3, 2)]
    peers += [at_z(1), at_z(7), sibling]
    for peer in peers:
        pl.semaphore_signal(barrier, inc=1, device_id=peer, device_id_type=MESH)
    pl.semaphore_wait(barrier, len(peers))

    def sems(ref, *lead):
        return lambda k: ref.at[(*lead, k)]

    def near_at(buf):
        return lambda i, part: buf.at[i] if part is None else buf.at[i, pl.ds(4 * part, 4)]

    def w_at(block, half):
        def at(i, part):
            first = half * 256 + (0 if part is None else 128 * part)
            return w_all.at[block(i), pl.ds(first, 256 if part is None else 128)]

        return at

    along_x = (x, at_xy(1, 0), at_xy(3, 0))
    along_y = (y, at_xy(0, 1), at_xy(0, 3))
    k1 = Ring4(near_at(k_near), *along_x, sems(kv1_send, 0), sems(kv1_recv, 0))
    v1 = Ring4(near_at(v_near), *along_y, sems(kv1_send, 1), sems(kv1_recv, 1))
    wa1 = Ring4(w_at(lambda i: i * 4 + y, 0), *along_x, sems(w1_send, 0), sems(w1_recv, 0))
    wb1 = Ring4(w_at(lambda i: x * 4 + i, 1), *along_y, sems(w1_send, 1), sems(w1_recv, 1))

    def offset(j):
        return j + j // 2 - 2 * (j // 3)

    def wa2(j):
        xs = (x + offset(j)) % 4
        return Ring4(w_at(lambda i: xs * 4 + i, 0), *along_y, sems(w2_send, 0, j), sems(w2_recv, 0, j))

    def wb2(j):
        ys = (y + offset(j)) % 4
        return Ring4(w_at(lambda i: i * 4 + ys, 1), *along_x, sems(w2_send, 1, j), sems(w2_recv, 1, j))

    def x_block(dz, part=None):
        block = ((z + dz) % 8) * 2 + core
        return x_all.at[block] if part is None else x_all.at[block, pl.ds(256 * part, 256)]

    def x_copy(way, k):
        dz = (8 - k) % 8 if way == 0 else k
        piece = x_block(dz, way if k == 3 else None)
        return remote(piece, piece, x_send.at[way, k], x_recv.at[way, k], at_z(1 if way == 0 else 7))

    def x_arrived(way, k):
        dz = (8 - k) % 8 if way == 0 else k
        piece = x_block(dz, way if k == 4 else None)
        remote(piece, piece, x_send.at[way, k - 1], x_recv.at[way, k - 1], at_z(1)).wait_recv()

    def pair_copy(way, k, other=False):
        dz = (8 - k) % 8 if way == 0 else k
        block = ((z + dz) % 8) * 2 + (1 - core if other else core)
        piece = x_all.at[block, pl.ds(256 * way, 256)] if k == 4 else x_all.at[block]
        return remote(piece, piece, pair_send.at[way, k], pair_recv.at[way, k], sibling)

    def x_step(k):
        for way in (0, 1):
            x_arrived(way, k)
            if k < 4:
                x_copy(way, k).start()
            pair_copy(way, k).start()

    def k2(r, d):
        return remote(
            k_send.at[(y + d) % 4, r], k_all.at[r, y],
            kv2_send.at[0, r, d - 1], kv2_recv.at[0, r, d - 1], at_xy(0, d),
        )

    def k2_arrived(r, d):
        remote(
            k_send.at[0, r], k_all.at[r, (y + 4 - d) % 4],
            kv2_send.at[0, r, d - 1], kv2_recv.at[0, r, d - 1], at_xy(0, d),
        ).wait_recv()

    def v2(r, d):
        return remote(
            v_send.at[(x + d) % 4, r], v_all.at[r, :, x],
            kv2_send.at[1, r, d - 1], kv2_recv.at[1, r, d - 1], at_xy(d, 0),
        )

    def v2_arrived(r, d):
        remote(
            v_send.at[0, r], v_all.at[r, :, (x + 4 - d) % 4],
            kv2_send.at[1, r, d - 1], kv2_recv.at[1, r, d - 1], at_xy(d, 0),
        ).wait_recv()

    loads[0].wait()
    loads[1].wait()
    k1.start()
    v1.start()
    loads[2].wait()
    x_copy(0, 0).start()
    x_copy(1, 0).start()
    pair_copy(0, 0).start()
    loads[3].wait()
    loads[4].wait()
    k1.forward()
    v1.forward()
    wa1.start()
    wb1.start()

    k1.finish()

    @pl.loop(0, REQS)
    def _(r):
        for yd in range(4):
            for xs in range(4):
                row = table[(x * 4 + yd) * REQS + r, xs * 4 + y]
                k_send[yd, r, xs] = k_near[xs, row]
        k_all[r, y] = k_send[y, r]
        for d in (1, 3, 2):
            k2(r, d).start()

    v1.finish()

    @pl.loop(0, REQS)
    def _(r):
        for xd in range(4):
            for ys in range(4):
                row = table[(xd * 4 + y) * REQS + r, x * 4 + ys]
                v_send[xd, r, ys] = v_near[ys, row]
        for ys in range(4):
            v_all[r, ys, x] = v_send[x, r, ys]
        for d in (1, 3, 2):
            v2(r, d).start()

    x_step(1)
    wa1.forward()
    wb1.forward()
    for j in (0, 1, 2):
        wa2(j).start()
        wb2(j).start()
    x_step(2)
    wa1.finish()
    wb1.finish()
    wa2(3).start()
    wb2(3).start()
    x_step(3)
    x_step(4)

    for way, k in ((0, 0), (0, 1), (1, 1), (0, 2), (1, 2), (0, 3), (1, 3), (0, 4), (1, 4)):
        pair_copy(way, k, other=True).wait_recv()

    squares[...] = jnp.zeros_like(squares)
    projected[...] = jnp.zeros_like(projected)

    @pl.loop(0, 16)
    def _(b):
        wide = x_all[b].astype(jnp.float32)
        wide = wide * wide
        squares[...] += (wide[:, 0:128] + wide[:, 128:256]) + (wide[:, 256:384] + wide[:, 384:512])

    def multiply(block, half):
        first = pl.multiple_of(half * 256, 256)
        projected[...] += dot(
            x_all[block, :, pl.ds(first, 256)], w_all[block, pl.ds(first, 256), :], NN
        )

    @pl.loop(0, REQS)
    def _(r):
        for d in (1, 3, 2):
            k2_arrived(r, d)
            v2_arrived(r, d)

        @pl.loop(0, QLEN // QTILE)
        def _(t):
            first = pl.multiple_of(t * QTILE, QTILE)
            shift = bias[r]
            for h in (0, 1):
                lanes = pl.ds(h * HD, HD)
                keys = k_all[r, :, :, :, lanes].reshape(SPAN, HD)
                values = v_all[r, :, :, :, lanes].reshape(SPAN, HD)
                scores = dot(q[r, pl.ds(first, QTILE), lanes], keys, NT) * TO_BASE_TWO + shift
                largest = jnp.max(scores, axis=-1, keepdims=True)
                exps = jnp.exp2(scores - largest)
                summed = jnp.sum(exps, axis=-1, keepdims=True)
                mixed[r, pl.ds(first, QTILE), lanes] = dot(exps.astype(jnp.bfloat16), values, NN)
                top[r, pl.ds(first, QTILE), lanes] = jnp.broadcast_to(largest, (QTILE, HD))
                total[r, pl.ds(first, QTILE), lanes] = jnp.broadcast_to(summed, (QTILE, HD))

        wa2(r).forward()
        wb2(r).forward()
        xs, ys = (x + offset(r)) % 4, (y + offset(r)) % 4

        @pl.loop(0, 3)
        def _(i):
            multiply(xs * 4 + (y + 3 + i) % 4, 0)
            multiply(((x + 3 + i) % 4) * 4 + ys, 1)

    @pl.loop(0, 4)
    def _(j):
        xs, ys = (x + offset(j)) % 4, (y + offset(j)) % 4
        wa2(j).finish()
        multiply(xs * 4 + (y + 2) % 4, 0)
        wb2(j).finish()
        multiply(((x + 2) % 4) * 4 + ys, 1)

    mean = jnp.sum(squares[...], axis=-1, keepdims=True) * (1.0 / D)
    fresh[...] = (projected[...] * lax.rsqrt(mean + EPS)).astype(jnp.bfloat16)

    @pl.loop(0, REQS)
    def _(r):
        rows = pl.ds(pl.multiple_of(r * SEL, SEL), SEL)
        for h in (0, 1):
            lanes = pl.ds(h * HD, HD)
            scores = dot(q[r, :, lanes], fresh[rows, lanes], NT) * TO_BASE_TWO
            before = top[r, :, lanes]
            largest = jnp.maximum(before, jnp.max(scores, axis=-1, keepdims=True))
            exps = jnp.exp2(scores - largest)
            fade = jnp.exp2(before - largest)
            summed = total[r, :, lanes] * fade + jnp.sum(exps, axis=-1, keepdims=True)
            gained = dot(exps.astype(jnp.bfloat16), fresh[rows, pl.ds(FEAT + h * HD, HD)], NN)
            attended = (mixed[r, :, lanes] * fade + gained) / summed
            result[r, :, lanes] = attended.astype(jnp.bfloat16)
        pltpu.make_async_copy(result.at[r], out_hbm.at[r], out_sem.at[r]).start()

    for ring in (k1, v1, wa1, wb1):
        ring.drain()

    @pl.loop(0, 4)
    def _(j):
        wa2(j).drain()
        wb2(j).drain()
        for d in (1, 2, 3):
            k2(j, d).wait_send()
            v2(j, d).wait_send()

    for way in (0, 1):
        for k in range(4):
            x_copy(way, k).wait_send()
    for way, k in ((0, 0), (0, 1), (1, 1), (0, 2), (1, 2), (0, 3), (1, 3), (0, 4), (1, 4)):
        pair_copy(way, k).wait_send()
    for r in range(REQS):
        pltpu.make_async_copy(result.at[r], out_hbm.at[r], out_sem.at[r]).wait()


def attend(q, kv, rows, weights, table, bias):
    any_ref = pl.BlockSpec(memory_space=pl.ANY)
    bf, f32 = jnp.bfloat16, jnp.float32
    dma = pltpu.SemaphoreType.DMA
    return pl.pallas_call(
        kernel,
        out_shape=jax.ShapeDtypeStruct((REQS, QLEN, FEAT), bf),
        in_specs=[any_ref] * 4
        + [pl.BlockSpec(memory_space=pltpu.SMEM), pl.BlockSpec(memory_space=pltpu.VMEM)],
        out_specs=any_ref,
        scratch_shapes=[
            pltpu.VMEM((REQS, QLEN, FEAT), bf),
            pltpu.VMEM((16, ROWS, DEEP), bf),
            pltpu.VMEM((16, DEEP, 2 * FEAT), bf),
            pltpu.VMEM((4, 8, BLK, FEAT), bf),
            pltpu.VMEM((4, 8, BLK, FEAT), bf),
            pltpu.VMEM((4, REQS, 4, BLK, FEAT), bf),
            pltpu.VMEM((4, REQS, 4, BLK, FEAT), bf),
            pltpu.VMEM((REQS, 4, 4, BLK, FEAT), bf),
            pltpu.VMEM((REQS, 4, 4, BLK, FEAT), bf),
            pltpu.VMEM((REQS, QLEN, FEAT), f32),
            pltpu.VMEM((REQS, QLEN, FEAT), f32),
            pltpu.VMEM((REQS, QLEN, FEAT), f32),
            pltpu.VMEM((ROWS, 2 * FEAT), f32),
            pltpu.VMEM((ROWS, HD), f32),
            pltpu.VMEM((ROWS, 2 * FEAT), bf),
            pltpu.VMEM((REQS, QLEN, FEAT), bf),
            dma((5,)),
            dma((REQS,)),
            dma((2, 4)), dma((2, 4)),
            dma((2, REQS, 3)), dma((2, REQS, 3)),
            dma((2, 4)), dma((2, 4)),
            dma((2, 4, 4)), dma((2, 4, 4)),
            dma((2, 4)), dma((2, 4)),
            dma((2, 5)), dma((2, 5)),
        ],
        compiler_params=pltpu.CompilerParams(
            collective_id=0, has_side_effects=True, vmem_limit_bytes=60 * 1024 * 1024
        ),
        cost_estimate=pl.CostEstimate(
            flops=14_000_000_000, bytes_accessed=8_000_000, transcendentals=10_000_000
        ),
        name="blend",
    )(q, kv, rows, weights, table, bias)


def local(
    queries, kv_store, hidden_rows, w_kv, passage_ids, passage_home, passage_counts, recompute_pos
):
    store = lax.axis_index("store")
    requests = passage_ids.shape[0]
    named = passage_ids[:, :, None] == jnp.arange(passage_home.shape[0])
    stored = jnp.sum(jnp.where(named, passage_home, 0), axis=-1)
    filled = (stored // 8)[:, :, None] == jnp.arange(16)
    slots = jnp.arange(SLOTS)[None, :, None]
    packed = jnp.sum(jnp.where(filled, slots * 8 + (stored % 8)[:, :, None], 0), axis=1)
    table = packed % 8
    mine = lax.dynamic_slice_in_dim(packed, store * REQS, REQS, 0) // 8
    counts = lax.dynamic_slice_in_dim(passage_counts, store * REQS, REQS, 0)
    mine = mine.reshape(REQS, 4, 4).transpose(0, 2, 1).reshape(REQS, SLOTS)
    place = (mine[:, :, None] * BLK + jnp.arange(BLK)).reshape(REQS, SPAN)
    renewed = jnp.any(place[:, None, :] == recompute_pos[:, :, None], axis=1)
    dropped = renewed | (place >= counts[:, None] * BLK)
    bias = jnp.where(dropped, MASKED, 0.0).astype(jnp.float32).reshape(REQS, 1, SPAN)
    return attend(
        queries,
        kv_store,
        hidden_rows.reshape(ROWS, DEEP),
        w_kv.reshape(DEEP, 2 * FEAT),
        table,
        bias,
    )


def solution(mesh):
    placed = (
        P("store", None, "head"),
        P("store", None, None, "head"),
        P("store", None, "head"),
        P("store", None, "head"),
        P(),
        P(),
        P(),
        P("store", None),
    )
    return jax.shard_map(
        local, mesh=mesh, in_specs=placed, out_specs=P("store", None, "head"), check_vma=False
    )
```

```python
import math

import jax
import jax.numpy as jnp
from jax import lax
from jax.experimental import pallas as pl
from jax.experimental.pallas import tpu as pltpu
from jax.sharding import PartitionSpec as P

MESH = pl.DeviceIdType.MESH

D = 8192
HD = 128
EPS = 1e-06
SLOTS = 16
BLK = 64
SPAN = SLOTS * BLK
REQS = 4
QLEN = 1024
SEL = 128
FEAT = 256
ROWS = REQS * SEL
DEEP = 512
QTILE = 256
MASKED = -1e30
TO_BASE_TWO = HD ** (-0.5) * math.log2(math.e)

NT = (((1,), (1,)), ((), ()))
NN = (((1,), (0,)), ((), ()))


def dot(a, b, dims):
    return lax.dot_general(a, b, dims, preferred_element_type=jnp.float32)


def remote(src, dst, send_sem, recv_sem, device):
    return pltpu.make_async_remote_copy(
        src_ref=src,
        dst_ref=dst,
        send_sem=send_sem,
        recv_sem=recv_sem,
        device_id=device,
        device_id_type=MESH,
    )


class Ring4:
    def __init__(self, at, me, plus, minus, send, recv):
        self.at, self.plus, self.minus, self.send, self.recv = at, plus, minus, send, recv
        self.me, self.prev, self.next, self.far = me, (me + 3) % 4, (me + 1) % 4, (me + 2) % 4

    def copy(self, source, part, k, device):
        piece = self.at(source, part)
        return remote(piece, piece, self.send(k), self.recv(k), device)

    def start(self):
        self.copy(self.me, None, 0, self.plus).start()
        self.copy(self.me, None, 1, self.minus).start()

    def forward(self):
        self.copy(self.prev, None, 0, self.plus).wait_recv()
        self.copy(self.prev, 0, 2, self.plus).start()
        self.copy(self.next, None, 1, self.minus).wait_recv()
        self.copy(self.next, 1, 3, self.minus).start()

    def finish(self):
        self.copy(self.far, 0, 2, self.plus).wait_recv()
        self.copy(self.far, 1, 3, self.minus).wait_recv()

    def drain(self):
        self.copy(self.me, None, 0, self.plus).wait_send()
        self.copy(self.me, None, 1, self.minus).wait_send()
        self.copy(self.prev, 0, 2, self.plus).wait_send()
        self.copy(self.next, 1, 3, self.minus).wait_send()


def kernel(
    q_hbm, kv_hbm, x_hbm, w_hbm, ids_hbm, home_hbm, counts_hbm, renewed_hbm, out_hbm,
    ids, home, counts, renewed, q, w_raw, packed, table, bias, x_all, w_all, k_near, v_near, k_send, v_send, k_all, v_all,
    mixed, top, total, projected, squares, fresh, result,
    local_sem, out_sem, kv1_send, kv1_recv, kv2_send, kv2_recv,
    w1_send, w1_recv, w2_send, w2_recv, x_send, x_recv, pair_send, pair_recv,
):
    store, head = lax.axis_index("store"), lax.axis_index("head")
    x, y, z, core = store // 4, store % 4, head // 2, head % 2

    def at_xy(dx, dy):
        return {"store": ((x + dx) % 4) * 4 + (y + dy) % 4, "head": head}

    def at_z(dz):
        return {"store": store, "head": ((z + dz) % 8) * 2 + core}

    sibling = {"store": store, "head": z * 2 + (1 - core)}

    loads = [
        pltpu.make_async_copy(kv_hbm.at[:, 0], k_near.at[x], local_sem.at[0]),
        pltpu.make_async_copy(kv_hbm.at[:, 1], v_near.at[y], local_sem.at[1]),
        pltpu.make_async_copy(x_hbm, x_all.at[head], local_sem.at[2]),
        pltpu.make_async_copy(w_hbm, w_raw, local_sem.at[3]),
        pltpu.make_async_copy(q_hbm, q, local_sem.at[4]),
        pltpu.make_async_copy(ids_hbm, ids, local_sem.at[5]),
        pltpu.make_async_copy(home_hbm, home, local_sem.at[6]),
        pltpu.make_async_copy(counts_hbm, counts, local_sem.at[7]),
        pltpu.make_async_copy(renewed_hbm, renewed, local_sem.at[8]),
    ]
    for load in loads:
        load.start()

    barrier = pltpu.get_barrier_semaphore()
    peers = [at_xy(d, 0) for d in (1, 3, 2)] + [at_xy(0, d) for d in (1, 3, 2)]
    peers += [at_z(1), at_z(7), sibling]
    for peer in peers:
        pl.semaphore_signal(barrier, inc=1, device_id=peer, device_id_type=MESH)
    pl.semaphore_wait(barrier, len(peers))

    def sems(ref, *lead):
        return lambda k: ref.at[(*lead, k)]

    def near_at(buf):
        return lambda i, part: buf.at[i] if part is None else buf.at[i, pl.ds(4 * part, 4)]

    def w_at(block, half):
        def at(i, part):
            first = half * 256 + (0 if part is None else 128 * part)
            return w_all.at[block(i), pl.ds(first, 256 if part is None else 128)]

        return at

    along_x = (x, at_xy(1, 0), at_xy(3, 0))
    along_y = (y, at_xy(0, 1), at_xy(0, 3))
    k1 = Ring4(near_at(k_near), *along_x, sems(kv1_send, 0), sems(kv1_recv, 0))
    v1 = Ring4(near_at(v_near), *along_y, sems(kv1_send, 1), sems(kv1_recv, 1))
    wa1 = Ring4(w_at(lambda i: i * 4 + y, 0), *along_x, sems(w1_send, 0), sems(w1_recv, 0))
    wb1 = Ring4(w_at(lambda i: x * 4 + i, 1), *along_y, sems(w1_send, 1), sems(w1_recv, 1))

    def offset(j):
        return j + j // 2 - 2 * (j // 3)

    def wa2(j):
        xs = (x + offset(j)) % 4
        return Ring4(w_at(lambda i: xs * 4 + i, 0), *along_y, sems(w2_send, 0, j), sems(w2_recv, 0, j))

    def wb2(j):
        ys = (y + offset(j)) % 4
        return Ring4(w_at(lambda i: i * 4 + ys, 1), *along_x, sems(w2_send, 1, j), sems(w2_recv, 1, j))

    def x_block(dz, part=None):
        block = ((z + dz) % 8) * 2 + core
        return x_all.at[block] if part is None else x_all.at[block, pl.ds(256 * part, 256)]

    def x_copy(way, k):
        dz = (8 - k) % 8 if way == 0 else k
        piece = x_block(dz, way if k == 3 else None)
        return remote(piece, piece, x_send.at[way, k], x_recv.at[way, k], at_z(1 if way == 0 else 7))

    def x_arrived(way, k):
        dz = (8 - k) % 8 if way == 0 else k
        piece = x_block(dz, way if k == 4 else None)
        remote(piece, piece, x_send.at[way, k - 1], x_recv.at[way, k - 1], at_z(1)).wait_recv()

    def pair_copy(way, k, other=False):
        dz = (8 - k) % 8 if way == 0 else k
        block = ((z + dz) % 8) * 2 + (1 - core if other else core)
        piece = x_all.at[block, pl.ds(256 * way, 256)] if k == 4 else x_all.at[block]
        return remote(piece, piece, pair_send.at[way, k], pair_recv.at[way, k], sibling)

    def x_step(k):
        for way in (0, 1):
            x_arrived(way, k)
            if k < 4:
                x_copy(way, k).start()
            pair_copy(way, k).start()

    def k2(r, d):
        return remote(
            k_send.at[(y + d) % 4, r], k_all.at[r, y],
            kv2_send.at[0, r, d - 1], kv2_recv.at[0, r, d - 1], at_xy(0, d),
        )

    def k2_arrived(r, d):
        remote(
            k_send.at[0, r], k_all.at[r, (y + 4 - d) % 4],
            kv2_send.at[0, r, d - 1], kv2_recv.at[0, r, d - 1], at_xy(0, d),
        ).wait_recv()

    def v2(r, d):
        return remote(
            v_send.at[(x + d) % 4, r], v_all.at[r, :, x],
            kv2_send.at[1, r, d - 1], kv2_recv.at[1, r, d - 1], at_xy(d, 0),
        )

    def v2_arrived(r, d):
        remote(
            v_send.at[0, r], v_all.at[r, :, (x + 4 - d) % 4],
            kv2_send.at[1, r, d - 1], kv2_recv.at[1, r, d - 1], at_xy(d, 0),
        ).wait_recv()

    def name_rows():
        named = ids[...]
        stored = lax.fori_loop(
            0, 128, lambda p, rows: jnp.where(named == p, home[p], rows), named, unroll=8
        )
        device = lax.broadcasted_iota(jnp.int32, (SLOTS, 64), 0)
        filled = jnp.zeros((SLOTS, 64), jnp.int32)
        for j in range(SLOTS):
            row = stored[j : j + 1, :]
            filled = jnp.where(device == (row >> 3), j * 8 + (row & 7), filled)
        packed[...] = jnp.zeros_like(packed)
        packed[:, pl.ds(0, 64)] = filled
        move = pltpu.make_async_copy(packed, table, local_sem.at[9])
        move.start()
        move.wait()

    def mask_positions():
        lane = lax.broadcasted_iota(jnp.int32, (1, SPAN), 1)
        block, inner = lane >> 6, lane & 63
        for r in range(REQS):
            mine = store * REQS + r
            place = jnp.zeros((1, SPAN), jnp.int32)
            for b in range(SLOTS):
                slot = table[(b % 4) * 4 + b // 4, mine] // 8
                place = jnp.where(block == b, slot * BLK, place)
            place = place + inner
            shift = jnp.where(place < counts[mine] * BLK, 0.0, MASKED)
            bias[r] = lax.fori_loop(
                0, SEL, lambda i, kept: jnp.where(place == renewed[r, i], MASKED, kept), shift, unroll=8
            )

    loads[0].wait()
    loads[1].wait()
    k1.start()
    v1.start()
    loads[2].wait()
    x_copy(0, 0).start()
    x_copy(1, 0).start()
    pair_copy(0, 0).start()
    loads[5].wait()
    loads[6].wait()
    name_rows()
    loads[3].wait()
    w_all[store, :, pl.ds(0, FEAT)] = w_raw[:, 0, :]
    w_all[store, :, pl.ds(FEAT, FEAT)] = w_raw[:, 1, :]
    k1.forward()
    v1.forward()
    wa1.start()
    wb1.start()

    k1.finish()

    @pl.loop(0, REQS)
    def _(r):
        for yd in range(4):
            for xs in range(4):
                row = table[xs * 4 + y, (x * 4 + yd) * REQS + r] % 8
                k_send[yd, r, xs] = k_near[xs, row]
        k_all[r, y] = k_send[y, r]
        for d in (1, 3, 2):
            k2(r, d).start()

    v1.finish()

    @pl.loop(0, REQS)
    def _(r):
        for xd in range(4):
            for ys in range(4):
                row = table[x * 4 + ys, (xd * 4 + y) * REQS + r] % 8
                v_send[xd, r, ys] = v_near[ys, row]
        for ys in range(4):
            v_all[r, ys, x] = v_send[x, r, ys]
        for d in (1, 3, 2):
            v2(r, d).start()

    x_step(1)
    wa1.forward()
    wb1.forward()
    for j in (0, 1, 2):
        wa2(j).start()
        wb2(j).start()
    x_step(2)
    wa1.finish()
    wb1.finish()
    wa2(3).start()
    wb2(3).start()
    x_step(3)
    x_step(4)

    for way, k in ((0, 0), (0, 1), (1, 1), (0, 2), (1, 2), (0, 3), (1, 3), (0, 4), (1, 4)):
        pair_copy(way, k, other=True).wait_recv()

    loads[4].wait()
    loads[7].wait()
    loads[8].wait()
    mask_positions()
    squares[...] = jnp.zeros_like(squares)
    projected[...] = jnp.zeros_like(projected)

    @pl.loop(0, 16)
    def _(b):
        wide = x_all[b].astype(jnp.float32)
        wide = wide * wide
        squares[...] += (wide[:, 0:128] + wide[:, 128:256]) + (wide[:, 256:384] + wide[:, 384:512])

    def multiply(block, half):
        first = pl.multiple_of(half * 256, 256)
        projected[...] += dot(
            x_all[block, :, pl.ds(first, 256)], w_all[block, pl.ds(first, 256), :], NN
        )

    @pl.loop(0, REQS)
    def _(r):
        for d in (1, 3, 2):
            k2_arrived(r, d)
            v2_arrived(r, d)

        @pl.loop(0, QLEN // QTILE)
        def _(t):
            first = pl.multiple_of(t * QTILE, QTILE)
            shift = bias[r]
            for h in (0, 1):
                lanes = pl.ds(h * HD, HD)
                keys = k_all[r, :, :, :, lanes].reshape(SPAN, HD)
                values = v_all[r, :, :, :, lanes].reshape(SPAN, HD)
                scores = dot(q[r, pl.ds(first, QTILE), lanes], keys, NT) * TO_BASE_TWO + shift
                largest = jnp.max(scores, axis=-1, keepdims=True)
                exps = jnp.exp2(scores - largest)
                summed = jnp.sum(exps, axis=-1, keepdims=True)
                mixed[r, pl.ds(first, QTILE), lanes] = dot(exps.astype(jnp.bfloat16), values, NN)
                top[r, pl.ds(first, QTILE), lanes] = jnp.broadcast_to(largest, (QTILE, HD))
                total[r, pl.ds(first, QTILE), lanes] = jnp.broadcast_to(summed, (QTILE, HD))

        wa2(r).forward()
        wb2(r).forward()
        xs, ys = (x + offset(r)) % 4, (y + offset(r)) % 4

        @pl.loop(0, 3)
        def _(i):
            multiply(xs * 4 + (y + 3 + i) % 4, 0)
            multiply(((x + 3 + i) % 4) * 4 + ys, 1)

    @pl.loop(0, 4)
    def _(j):
        xs, ys = (x + offset(j)) % 4, (y + offset(j)) % 4
        wa2(j).finish()
        multiply(xs * 4 + (y + 2) % 4, 0)
        wb2(j).finish()
        multiply(((x + 2) % 4) * 4 + ys, 1)

    mean = jnp.sum(squares[...], axis=-1, keepdims=True) * (1.0 / D)
    fresh[...] = (projected[...] * lax.rsqrt(mean + EPS)).astype(jnp.bfloat16)

    @pl.loop(0, REQS)
    def _(r):
        rows = pl.ds(pl.multiple_of(r * SEL, SEL), SEL)
        for h in (0, 1):
            lanes = pl.ds(h * HD, HD)
            scores = dot(q[r, :, lanes], fresh[rows, lanes], NT) * TO_BASE_TWO
            before = top[r, :, lanes]
            largest = jnp.maximum(before, jnp.max(scores, axis=-1, keepdims=True))
            exps = jnp.exp2(scores - largest)
            fade = jnp.exp2(before - largest)
            summed = total[r, :, lanes] * fade + jnp.sum(exps, axis=-1, keepdims=True)
            gained = dot(exps.astype(jnp.bfloat16), fresh[rows, pl.ds(FEAT + h * HD, HD)], NN)
            attended = (mixed[r, :, lanes] * fade + gained) / summed
            result[r, :, lanes] = attended.astype(jnp.bfloat16)
        pltpu.make_async_copy(result.at[r], out_hbm.at[r], out_sem.at[r]).start()

    for ring in (k1, v1, wa1, wb1):
        ring.drain()

    @pl.loop(0, 4)
    def _(j):
        wa2(j).drain()
        wb2(j).drain()
        for d in (1, 2, 3):
            k2(j, d).wait_send()
            v2(j, d).wait_send()

    for way in (0, 1):
        for k in range(4):
            x_copy(way, k).wait_send()
    for way, k in ((0, 0), (0, 1), (1, 1), (0, 2), (1, 2), (0, 3), (1, 3), (0, 4), (1, 4)):
        pair_copy(way, k).wait_send()
    for r in range(REQS):
        pltpu.make_async_copy(result.at[r], out_hbm.at[r], out_sem.at[r]).wait()


def attend(q, kv, rows, weights, ids, home, counts, renewed):
    hbm = pl.BlockSpec(memory_space=pltpu.HBM)
    bf, f32 = jnp.bfloat16, jnp.float32
    dma = pltpu.SemaphoreType.DMA
    return pl.pallas_call(
        kernel,
        out_shape=jax.ShapeDtypeStruct((REQS, QLEN, FEAT), bf),
        in_specs=[hbm] * 8,
        out_specs=pl.BlockSpec(memory_space=pl.ANY),
        scratch_shapes=[
            pltpu.VMEM((SLOTS, 64), jnp.int32),
            pltpu.SMEM((128,), jnp.int32),
            pltpu.SMEM((64,), jnp.int32),
            pltpu.SMEM((REQS, SEL), jnp.int32),
            pltpu.VMEM((REQS, QLEN, FEAT), bf),
            pltpu.VMEM((DEEP, 2, FEAT), bf),
            pltpu.VMEM((SLOTS, 128), jnp.int32),
            pltpu.SMEM((SLOTS, 128), jnp.int32),
            pltpu.VMEM((REQS, 1, SPAN), f32),
            pltpu.VMEM((16, ROWS, DEEP), bf),
            pltpu.VMEM((16, DEEP, 2 * FEAT), bf),
            pltpu.VMEM((4, 8, BLK, FEAT), bf),
            pltpu.VMEM((4, 8, BLK, FEAT), bf),
            pltpu.VMEM((4, REQS, 4, BLK, FEAT), bf),
            pltpu.VMEM((4, REQS, 4, BLK, FEAT), bf),
            pltpu.VMEM((REQS, 4, 4, BLK, FEAT), bf),
            pltpu.VMEM((REQS, 4, 4, BLK, FEAT), bf),
            pltpu.VMEM((REQS, QLEN, FEAT), f32),
            pltpu.VMEM((REQS, QLEN, FEAT), f32),
            pltpu.VMEM((REQS, QLEN, FEAT), f32),
            pltpu.VMEM((ROWS, 2 * FEAT), f32),
            pltpu.VMEM((ROWS, HD), f32),
            pltpu.VMEM((ROWS, 2 * FEAT), bf),
            pltpu.VMEM((REQS, QLEN, FEAT), bf),
            dma((10,)),
            dma((REQS,)),
            dma((2, 4)), dma((2, 4)),
            dma((2, REQS, 3)), dma((2, REQS, 3)),
            dma((2, 4)), dma((2, 4)),
            dma((2, 4, 4)), dma((2, 4, 4)),
            dma((2, 4)), dma((2, 4)),
            dma((2, 5)), dma((2, 5)),
        ],
        compiler_params=pltpu.CompilerParams(
            collective_id=0, has_side_effects=True, vmem_limit_bytes=60 * 1024 * 1024
        ),
        cost_estimate=pl.CostEstimate(
            flops=14_000_000_000, bytes_accessed=8_000_000, transcendentals=10_000_000
        ),
        name="blend",
    )(q, kv, rows, weights, ids, home, counts, renewed)


def local(
    queries, kv_store, hidden_rows, w_kv, passage_ids, passage_home, passage_counts, recompute_pos
):
    return attend(
        queries,
        kv_store,
        hidden_rows.reshape(ROWS, DEEP),
        w_kv,
        passage_ids.T,
        passage_home,
        passage_counts,
        recompute_pos,
    )


def solution(mesh):
    placed = (
        P("store", None, "head"),
        P("store", None, None, "head"),
        P("store", None, "head"),
        P("store", None, "head"),
        P(),
        P(),
        P(),
        P("store", None),
    )
    return jax.shard_map(
        local, mesh=mesh, in_specs=placed, out_specs=P("store", None, "head"), check_vma=False
    )
```

```python
import math

import jax
import jax.numpy as jnp
from jax import lax
from jax.experimental import pallas as pl
from jax.experimental.pallas import tpu as pltpu
from jax.sharding import PartitionSpec as P

MESH = pl.DeviceIdType.MESH

D = 8192
HD = 128
EPS = 1e-06
SLOTS = 16
BLK = 64
SPAN = SLOTS * BLK
REQS = 4
QLEN = 1024
SEL = 128
FEAT = 256
ROWS = REQS * SEL
DEEP = 512
QTILE = 256
MASKED = -1e28
TO_BASE_TWO = HD ** (-0.5) * math.log2(math.e)

NT = (((1,), (1,)), ((), ()))
NN = (((1,), (0,)), ((), ()))


def dot(a, b, dims):
    return lax.dot_general(a, b, dims, preferred_element_type=jnp.float32)


def remote(src, dst, send_sem, recv_sem, device):
    return pltpu.make_async_remote_copy(
        src_ref=src,
        dst_ref=dst,
        send_sem=send_sem,
        recv_sem=recv_sem,
        device_id=device,
        device_id_type=MESH,
    )


class Ring4:
    def __init__(self, at, me, plus, minus, send, recv):
        self.at, self.plus, self.minus, self.send, self.recv = at, plus, minus, send, recv
        self.me, self.prev, self.next, self.far = me, (me + 3) % 4, (me + 1) % 4, (me + 2) % 4

    def copy(self, source, part, k, device):
        piece = self.at(source, part)
        return remote(piece, piece, self.send(k), self.recv(k), device)

    def start(self):
        self.copy(self.me, None, 0, self.plus).start()
        self.copy(self.me, None, 1, self.minus).start()

    def forward(self):
        self.copy(self.prev, None, 0, self.plus).wait_recv()
        self.copy(self.prev, 0, 2, self.plus).start()
        self.copy(self.next, None, 1, self.minus).wait_recv()
        self.copy(self.next, 1, 3, self.minus).start()

    def finish(self):
        self.copy(self.far, 0, 2, self.plus).wait_recv()
        self.copy(self.far, 1, 3, self.minus).wait_recv()

    def drain(self):
        self.copy(self.me, None, 0, self.plus).wait_send()
        self.copy(self.me, None, 1, self.minus).wait_send()
        self.copy(self.prev, 0, 2, self.plus).wait_send()
        self.copy(self.next, 1, 3, self.minus).wait_send()


def kernel(
    q_hbm, kv_hbm, x_hbm, w_hbm, ids_hbm, home_hbm, counts_hbm, renewed_hbm, out_hbm,
    ids, home, counts, renewed, q, w_raw, packed, table, bias, x_own, x_all, w_all, k_near, v_near, k_send, v_send, k_all, v_all,
    mixed, top, total, projected, squares, part_send, part_recv, norm_send, norm_recv, fresh, result,
    wide_q, wide_k, wide_v,
    local_sem, out_sem, kv1_send, kv1_recv, kv2_send, kv2_recv,
    own_send, own_recv, other_send, other_recv, side_send, side_recv, flow_send, flow_recv,
    lend_send, lend_recv, core_send, core_recv, sum_send, sum_recv,
):
    store, head = lax.axis_index("store"), lax.axis_index("head")
    x, y, z, core = store // 4, store % 4, head // 2, head % 2

    def at_xy(dx, dy):
        return {"store": ((x + dx) % 4) * 4 + (y + dy) % 4, "head": head}

    def at_z(dz):
        return {"store": store, "head": ((z + dz) % 8) * 2 + core}

    sibling = {"store": store, "head": z * 2 + (1 - core)}

    half_of, odd = y // 2, y % 2
    source = z % 2 == half_of
    relay = z % 2 != half_of
    ally = {"store": x * 4 + y + 1 - 2 * odd, "head": head}
    partner = {"store": x * 4 + 3 - y, "head": head}
    x_mine = (z // 2) * 2 + core
    w_mine = x * 2 + odd

    loads = [
        pltpu.make_async_copy(kv_hbm.at[:, 0], k_near.at[x], local_sem.at[0]),
        pltpu.make_async_copy(kv_hbm.at[:, 1], v_near.at[y], local_sem.at[1]),
        pltpu.make_async_copy(w_hbm, w_raw, local_sem.at[3]),
        pltpu.make_async_copy(q_hbm, q, local_sem.at[4]),
        pltpu.make_async_copy(ids_hbm, ids, local_sem.at[5]),
        pltpu.make_async_copy(home_hbm, home, local_sem.at[6]),
        pltpu.make_async_copy(counts_hbm, counts, local_sem.at[7]),
        pltpu.make_async_copy(renewed_hbm, renewed, local_sem.at[8]),
    ]
    for load in loads:
        load.start()
    x_load = pltpu.make_async_copy(x_hbm, x_all.at[x_mine, pl.ds(0, ROWS)], local_sem.at[2])
    x_lent = pltpu.make_async_copy(x_hbm, x_own, local_sem.at[2])
    pl.when(source)(x_load.start)
    pl.when(relay)(x_lent.start)

    barrier = pltpu.get_barrier_semaphore()
    peers = [at_xy(d, 0) for d in (1, 3, 2)] + [at_xy(0, d) for d in (1, 3, 2)]
    peers += [at_z(1), at_z(7), sibling]
    for peer in peers:
        pl.semaphore_signal(barrier, inc=1, device_id=peer, device_id_type=MESH)
    pl.semaphore_wait(barrier, len(peers))

    def sems(ref, *lead):
        return lambda k: ref.at[(*lead, k)]

    def near_at(buf):
        return lambda i, part: buf.at[i] if part is None else buf.at[i, pl.ds(4 * part, 4)]

    def w_at(side, first, rows):
        def at(i, part):
            if part is None:
                return w_all.at[i * 2 + side, pl.ds(first, rows)]
            return w_all.at[i * 2 + side, pl.ds(first + part * (rows // 2), rows // 2)]

        return at

    along_x = (x, at_xy(1, 0), at_xy(3, 0))
    along_y = (y, at_xy(0, 1), at_xy(0, 3))
    k1 = Ring4(near_at(k_near), *along_x, sems(kv1_send, 0), sems(kv1_recv, 0))
    v1 = Ring4(near_at(v_near), *along_y, sems(kv1_send, 1), sems(kv1_recv, 1))
    own = Ring4(w_at(odd, 0, DEEP), *along_x, sems(own_send), sems(own_recv))
    other = Ring4(w_at(1 - odd, 0, DEEP // 2), *along_x, sems(other_send), sems(other_recv))

    def offset(j):
        return j + j // 2 - 2 * (j // 3)

    def side(j, sent=True):
        block = (x + offset(j % 4)) % 4 * 2 + (odd if sent else 1 - odd)
        piece = w_all.at[block, pl.ds(0 if j == 4 else DEEP // 2, DEEP // 2)]
        return remote(piece, piece, side_send.at[j], side_recv.at[j], ally)

    def x_piece(way, dist, w):
        at = (z + (8 - dist if way == 0 else dist)) % 8
        return x_all.at[(at // 2) * 2 + core, pl.ds(256 * w, 256)]

    def flow(way, stage, dist, w):
        piece = x_piece(way, dist, w)
        device = at_z(1 if way == 0 else 7)
        return remote(piece, piece, flow_send.at[way, stage, w], flow_recv.at[way, stage, w], device)

    def lend(half):
        return remote(
            x_own.at[pl.ds(256 * half, 256)], x_all.at[x_mine, pl.ds(ROWS + 256 * half, 256)],
            lend_send.at[half], lend_recv.at[half], partner,
        )

    def to_core(dist, part, mine=True):
        at = (z + 8 + dist) % 8
        piece = x_all.at[(at // 2) * 2 + (core if mine else 1 - core), pl.ds(ROWS * part, ROWS)]
        return remote(piece, piece, core_send.at[at // 2, part], core_recv.at[at // 2, part], sibling)

    def x_start():
        @pl.when(source)
        def _():
            x_load.wait()
            for w in (0, 1):
                flow(0, 0, 0, w).start()
                flow(1, 0, 0, w).start()
            to_core(0, 0).start()

        @pl.when(relay)
        def _():
            x_lent.wait()
            lend(0).start()
            lend(1).start()

    def x_one():
        @pl.when(relay)
        def _():
            for w in (0, 1):
                for way in (0, 1):
                    flow(way, 0, 1, w).wait_recv()
                    flow(way, 0, 1, w).start()
            to_core(-1, 0).start()
            to_core(1, 0).start()

        @pl.when(source)
        def _():
            for w in (2, 3):
                lend(w - 2).wait_recv()
                flow(0, 0, 0, w).start()
                flow(1, 0, 0, w).start()
            to_core(0, 1).start()

    def x_two(half):
        w = 2 + half

        @pl.when(relay)
        def _():
            for way in (0, 1):
                flow(way, 0, 1, w).wait_recv()
                flow(way, 0, 1, w).start()
            if half:
                to_core(-1, 1).start()
                to_core(1, 1).start()

        @pl.when(source)
        def _():
            for way in (0, 1):
                flow(way, 0, 2, half).wait_recv()
            if half:
                to_core(-2, 0).start()
                to_core(2, 0).start()

    def x_three(half):
        w = 2 + half

        @pl.when(source)
        def _():
            for way in (0, 1):
                flow(way, 0, 2, w).wait_recv()
                flow(way, 1, 2, w).start()
            if half:
                for way in (0, 1):
                    flow(way, 1, 2, 0).start()
                    flow(way, 1, 2, 1).start()
                to_core(-2, 1).start()
                to_core(2, 1).start()

    def x_relayed(part):
        @pl.when(relay)
        def _():
            for half in (0, 1):
                w = 2 * part + half
                for way in (0, 1):
                    flow(way, 1, 3, w).wait_recv()
                    if way == half:
                        flow(way, 1, 3, w).start()
            to_core(-3, part).start()
            to_core(3, part).start()

    def x_ended(part):
        @pl.when(source)
        def _():
            for way in (0, 1):
                flow(way, 1, 4, 2 * part + way).wait_recv()
            to_core(4, part).start()

    def x_others(part):
        for at in range(4):
            piece = x_all.at[at * 2 + 1 - core, pl.ds(ROWS * part, ROWS)]
            remote(piece, piece, core_send.at[at, part], core_recv.at[at, part], sibling).wait_recv()

    def x_drain():
        @pl.when(source)
        def _():
            for way in (0, 1):
                for w in range(4):
                    flow(way, 0, 0, w).wait_send()
                    flow(way, 1, 2, w).wait_send()

        @pl.when(relay)
        def _():
            lend(0).wait_send()
            lend(1).wait_send()
            for way in (0, 1):
                for w in range(4):
                    flow(way, 0, 1, w).wait_send()
                for part in (0, 1):
                    flow(way, 1, 3, 2 * part + way).wait_send()

        for at in range(4):
            for part in (0, 1):
                piece = x_all.at[at * 2 + core, pl.ds(ROWS * part, ROWS)]
                remote(piece, piece, core_send.at[at, part], core_recv.at[at, part], sibling).wait_send()

    swap = remote(part_send, part_recv, sum_send.at[0], sum_recv.at[0], partner)
    swap_norm = remote(norm_send, norm_recv, sum_send.at[1], sum_recv.at[1], partner)

    def k2(r, d):
        return remote(
            k_send.at[(y + d) % 4, r], k_all.at[r, y],
            kv2_send.at[0, r, d - 1], kv2_recv.at[0, r, d - 1], at_xy(0, d),
        )

    def k2_arrived(r, d):
        remote(
            k_send.at[0, r], k_all.at[r, (y + 4 - d) % 4],
            kv2_send.at[0, r, d - 1], kv2_recv.at[0, r, d - 1], at_xy(0, d),
        ).wait_recv()

    def v2(r, d):
        return remote(
            v_send.at[(x + d) % 4, r], v_all.at[r, :, x],
            kv2_send.at[1, r, d - 1], kv2_recv.at[1, r, d - 1], at_xy(d, 0),
        )

    def v2_arrived(r, d):
        remote(
            v_send.at[0, r], v_all.at[r, :, (x + 4 - d) % 4],
            kv2_send.at[1, r, d - 1], kv2_recv.at[1, r, d - 1], at_xy(d, 0),
        ).wait_recv()

    def name_rows():
        named = ids[...]
        stored = lax.fori_loop(
            0, 128, lambda p, rows: jnp.where(named == p, home[p], rows), named, unroll=8
        )
        device = lax.broadcasted_iota(jnp.int32, (SLOTS, 64), 0)
        filled = jnp.zeros((SLOTS, 64), jnp.int32)
        for j in range(SLOTS):
            row = stored[j : j + 1, :]
            filled = jnp.where(device == (row >> 3), j * 8 + (row & 7), filled)
        packed[...] = jnp.zeros_like(packed)
        packed[:, pl.ds(0, 64)] = filled
        move = pltpu.make_async_copy(packed, table, local_sem.at[9])
        move.start()
        move.wait()

    def mask_positions():
        lane = lax.broadcasted_iota(jnp.int32, (1, SPAN), 1)
        block, inner = lane >> 6, lane & 63
        for r in range(REQS):
            mine = store * REQS + r
            place = jnp.zeros((1, SPAN), jnp.int32)
            for b in range(SLOTS):
                slot = table[(b % 4) * 4 + b // 4, mine] // 8
                place = jnp.where(block == b, slot * BLK, place)
            place = place + inner
            shift = jnp.where(place < counts[mine] * BLK, 0.0, MASKED)
            bias[r] = lax.fori_loop(
                0, SEL, lambda i, kept: jnp.where(place == renewed[r, i], MASKED, kept), shift, unroll=8
            )

    def send_keys(first, count):
        @pl.loop(first, first + count)
        def _(r):
            for yd in range(4):
                for xs in range(4):
                    row = table[xs * 4 + y, (x * 4 + yd) * REQS + r] % 8
                    k_send[yd, r, xs] = k_near[xs, row]
            k_all[r, y] = k_send[y, r]
            for d in (1, 3, 2):
                k2(r, d).start()

    def send_values(first, count):
        @pl.loop(first, first + count)
        def _(r):
            for xd in range(4):
                for ys in range(4):
                    row = table[x * 4 + ys, (xd * 4 + y) * REQS + r] % 8
                    v_send[xd, r, ys] = v_near[ys, row]
            for ys in range(4):
                v_all[r, ys, x] = v_send[x, r, ys]
            for d in (1, 3, 2):
                v2(r, d).start()

    def attend_cached(r):
        for d in (1, 3, 2):
            k2_arrived(r, d)
            v2_arrived(r, d)

        @pl.loop(0, QLEN // QTILE)
        def _(t):
            first = pl.multiple_of(t * QTILE, QTILE)
            shift = bias[r]
            for h in (0, 1):
                lanes = pl.ds(h * HD, HD)
                keys = k_all[r, :, :, :, lanes].reshape(SPAN, HD)
                values = v_all[r, :, :, :, lanes].reshape(SPAN, HD)
                scores = dot(q[r, pl.ds(first, QTILE), lanes], keys, NT) * TO_BASE_TWO + shift
                largest = jnp.max(scores, axis=-1, keepdims=True)
                exps = jnp.exp2(scores - largest)
                summed = jnp.sum(exps, axis=-1, keepdims=True)
                mixed[r, pl.ds(first, QTILE), lanes] = dot(exps.astype(jnp.bfloat16), values, NN)
                top[r, pl.ds(first, QTILE), lanes] = jnp.broadcast_to(largest, (QTILE, HD))
                total[r, pl.ds(first, QTILE), lanes] = jnp.broadcast_to(summed, (QTILE, HD))

    def project(part):
        projected[...] = jnp.zeros_like(projected)

        @pl.loop(0, 8)
        def _(b):
            projected[...] += dot(x_all[b, pl.ds(ROWS * part, ROWS), :], w_all[b], NN)

    x_start()
    loads[0].wait()
    k1.start()
    loads[1].wait()
    v1.start()
    loads[2].wait()
    w_all[w_mine, :, pl.ds(0, FEAT)] = w_raw[:, 0, :]
    w_all[w_mine, :, pl.ds(FEAT, FEAT)] = w_raw[:, 1, :]
    side(4).start()
    loads[4].wait()
    loads[5].wait()
    name_rows()
    k1.forward()
    own.start()
    side(0).start()
    k1.finish()
    send_keys(0, 1)
    x_one()
    v1.forward()
    side(4, False).wait_recv()
    other.start()
    x_two(0)
    own.forward()
    side(1).start()
    side(2).start()
    x_two(1)
    v1.finish()
    send_values(0, 1)
    x_three(0)
    loads[3].wait()
    loads[6].wait()
    loads[7].wait()
    mask_positions()
    other.forward()
    x_three(1)
    own.finish()
    side(3).start()
    send_keys(1, 3)
    send_values(1, 3)
    x_relayed(1)
    attend_cached(0)
    x_ended(1)
    other.finish()
    for j in range(4):
        side(j, False).wait_recv()
    x_others(1)

    norm_send[...] = jnp.zeros_like(norm_send)

    @pl.loop(0, 8)
    def _(b):
        narrow = x_all[b, pl.ds(ROWS, ROWS), :]
        norm_send[...] += dot(jnp.ones((8, DEEP), jnp.bfloat16), narrow * narrow, NT)

    project(1)
    part_send[...] = projected[...].astype(jnp.bfloat16)
    swap.start()
    swap_norm.start()
    x_relayed(0)
    attend_cached(1)
    x_ended(0)
    x_others(0)
    squares[...] = jnp.zeros_like(squares)

    @pl.loop(0, 8)
    def _(b):
        wide = x_all[b, pl.ds(0, ROWS), :].astype(jnp.float32)
        wide = wide * wide
        squares[...] += (wide[:, 0:128] + wide[:, 128:256]) + (wide[:, 256:384] + wide[:, 384:512])

    project(0)

    @pl.loop(2, REQS)
    def _(r):
        attend_cached(r)

    swap.wait_recv()
    swap_norm.wait_recv()
    lent = jnp.transpose(jnp.broadcast_to(norm_recv[0:1, :], (HD, ROWS)))
    mean = (jnp.sum(squares[...], axis=-1, keepdims=True) + lent) * (1.0 / D)
    scale = lax.rsqrt(mean + EPS)
    for i in range(4):
        lanes = pl.ds(i * HD, HD)
        summed = projected[:, lanes] + part_recv[:, lanes].astype(jnp.float32)
        at = i * HD if i < 2 else FEAT + (i - 2) * 2 * HD
        fresh[:, pl.ds(at, HD)] = (summed * scale).astype(jnp.bfloat16)
        if i >= 2:
            fresh[:, pl.ds(at + HD, HD)] = jnp.ones((ROWS, HD), jnp.bfloat16)

    @pl.loop(0, REQS)
    def _(r):
        rows = pl.ds(pl.multiple_of(r * SEL, SEL), SEL)
        for h in (0, 1):
            lanes = pl.ds(h * HD, HD)
            scores = dot(q[r, :, lanes], fresh[rows, lanes], NT) * TO_BASE_TWO
            before = top[r, :, lanes]
            largest = jnp.maximum(before, jnp.max(scores, axis=-1, keepdims=True))
            exps = jnp.exp2(scores - largest)
            fade = jnp.exp2(before - largest)
            both = dot(exps.astype(jnp.bfloat16), fresh[rows, pl.ds(FEAT + h * 2 * HD, 2 * HD)], NN)
            attended = (mixed[r, :, lanes] * fade + both[:, 0:HD]) / (total[r, :, lanes] * fade + both[:, HD:])
            result[r, :, lanes] = attended.astype(jnp.bfloat16)
        pltpu.make_async_copy(result.at[r], out_hbm.at[r], out_sem.at[r]).start()

    for ring in (k1, v1, own, other):
        ring.drain()
    for j in range(5):
        side(j).wait_send()

    @pl.loop(0, REQS)
    def _(r):
        for d in (1, 2, 3):
            k2(r, d).wait_send()
            v2(r, d).wait_send()

    x_drain()
    swap.wait_send()
    swap_norm.wait_send()
    for r in range(REQS):
        pltpu.make_async_copy(result.at[r], out_hbm.at[r], out_sem.at[r]).wait()


def attend(q, kv, rows, weights, ids, home, counts, renewed):
    hbm = pl.BlockSpec(memory_space=pltpu.HBM)
    bf, f32 = jnp.bfloat16, jnp.float32
    dma = pltpu.SemaphoreType.DMA
    return pl.pallas_call(
        kernel,
        out_shape=jax.ShapeDtypeStruct((REQS, QLEN, FEAT), bf),
        in_specs=[hbm] * 8,
        out_specs=pl.BlockSpec(memory_space=pl.ANY),
        scratch_shapes=[
            pltpu.VMEM((SLOTS, 64), jnp.int32),
            pltpu.SMEM((128,), jnp.int32),
            pltpu.SMEM((64,), jnp.int32),
            pltpu.SMEM((REQS, SEL), jnp.int32),
            pltpu.VMEM((REQS, QLEN, FEAT), bf),
            pltpu.VMEM((DEEP, 2, FEAT), bf),
            pltpu.VMEM((SLOTS, 128), jnp.int32),
            pltpu.SMEM((SLOTS, 128), jnp.int32),
            pltpu.VMEM((REQS, 1, SPAN), f32),
            pltpu.VMEM((ROWS, DEEP), bf),
            pltpu.VMEM((8, 2 * ROWS, DEEP), bf),
            pltpu.VMEM((8, DEEP, 2 * FEAT), bf),
            pltpu.VMEM((4, 8, BLK, FEAT), bf),
            pltpu.VMEM((4, 8, BLK, FEAT), bf),
            pltpu.VMEM((4, REQS, 4, BLK, FEAT), bf),
            pltpu.VMEM((4, REQS, 4, BLK, FEAT), bf),
            pltpu.VMEM((REQS, 4, 4, BLK, FEAT), bf),
            pltpu.VMEM((REQS, 4, 4, BLK, FEAT), bf),
            pltpu.VMEM((REQS, QLEN, FEAT), f32),
            pltpu.VMEM((REQS, QLEN, FEAT), f32),
            pltpu.VMEM((REQS, QLEN, FEAT), f32),
            pltpu.VMEM((ROWS, 2 * FEAT), f32),
            pltpu.VMEM((ROWS, HD), f32),
            pltpu.VMEM((ROWS, 2 * FEAT), bf),
            pltpu.VMEM((ROWS, 2 * FEAT), bf),
            pltpu.VMEM((8, ROWS), f32),
            pltpu.VMEM((8, ROWS), f32),
            pltpu.VMEM((ROWS, 3 * FEAT), bf),
            pltpu.VMEM((REQS, QLEN, FEAT), bf),
            pltpu.VMEM((2, QLEN, 2 * HD), bf),
            pltpu.VMEM((2, SPAN, 2 * HD), bf),
            pltpu.VMEM((2, SPAN, 2 * HD), bf),
            dma((11,)),
            dma((REQS,)),
            dma((2, 4)), dma((2, 4)),
            dma((2, REQS, 3)), dma((2, REQS, 3)),
            dma((4,)), dma((4,)),
            dma((4,)), dma((4,)),
            dma((5,)), dma((5,)),
            dma((2, 2, 4)), dma((2, 2, 4)),
            dma((2,)), dma((2,)),
            dma((4, 2)), dma((4, 2)),
            dma((2,)), dma((2,)),
        ],
        compiler_params=pltpu.CompilerParams(
            collective_id=0, has_side_effects=True, vmem_limit_bytes=60 * 1024 * 1024
        ),
        cost_estimate=pl.CostEstimate(
            flops=14_000_000_000, bytes_accessed=8_000_000, transcendentals=10_000_000
        ),
        name="blend",
    )(q, kv, rows, weights, ids, home, counts, renewed)


def local(
    queries, kv_store, hidden_rows, w_kv, passage_ids, passage_home, passage_counts, recompute_pos
):
    return attend(
        queries,
        kv_store,
        hidden_rows.reshape(ROWS, DEEP),
        w_kv,
        passage_ids.T,
        passage_home,
        passage_counts,
        recompute_pos,
    )


def solution(mesh):
    placed = (
        P("store", None, "head"),
        P("store", None, None, "head"),
        P("store", None, "head"),
        P("store", None, "head"),
        P(),
        P(),
        P(),
        P("store", None),
    )
    return jax.shard_map(
        local, mesh=mesh, in_specs=placed, out_specs=P("store", None, "head"), check_vma=False
    )
```

```python
import math

import jax
import jax.numpy as jnp
from jax import lax
from jax.experimental import pallas as pl
from jax.experimental.pallas import tpu as pltpu
from jax.sharding import PartitionSpec as P

MESH = pl.DeviceIdType.MESH

D = 8192
HD = 128
EPS = 1e-06
SLOTS = 16
BLK = 64
SPAN = SLOTS * BLK
REQS = 4
QLEN = 1024
SEL = 128
FEAT = 256
ROWS = REQS * SEL
DEEP = 512
QTILE = 512
MASKED = -1e28
TO_BASE_TWO = HD ** (-0.5) * math.log2(math.e)

NT = (((1,), (1,)), ((), ()))
NN = (((1,), (0,)), ((), ()))


def dot(a, b, dims):
    return lax.dot_general(a, b, dims, preferred_element_type=jnp.float32)


def remote(src, dst, send_sem, recv_sem, device):
    return pltpu.make_async_remote_copy(
        src_ref=src,
        dst_ref=dst,
        send_sem=send_sem,
        recv_sem=recv_sem,
        device_id=device,
        device_id_type=MESH,
    )


class Ring4:
    def __init__(self, at, me, plus, minus, send, recv):
        self.at, self.plus, self.minus, self.send, self.recv = at, plus, minus, send, recv
        self.me, self.prev, self.next, self.far = me, (me + 3) % 4, (me + 1) % 4, (me + 2) % 4

    def copy(self, source, part, k, device):
        piece = self.at(source, part)
        return remote(piece, piece, self.send(k), self.recv(k), device)

    def start(self):
        self.copy(self.me, None, 0, self.plus).start()
        self.copy(self.me, None, 1, self.minus).start()

    def forward(self):
        self.copy(self.prev, None, 0, self.plus).wait_recv()
        self.copy(self.prev, 0, 2, self.plus).start()
        self.copy(self.next, None, 1, self.minus).wait_recv()
        self.copy(self.next, 1, 3, self.minus).start()

    def finish(self):
        self.copy(self.far, 0, 2, self.plus).wait_recv()
        self.copy(self.far, 1, 3, self.minus).wait_recv()

    def drain(self):
        self.copy(self.me, None, 0, self.plus).wait_send()
        self.copy(self.me, None, 1, self.minus).wait_send()
        self.copy(self.prev, 0, 2, self.plus).wait_send()
        self.copy(self.next, 1, 3, self.minus).wait_send()


def kernel(
    q_hbm, kv_hbm, x_hbm, w_hbm, ids_hbm, home_hbm, counts_hbm, renewed_hbm, out_hbm,
    ids, home, counts, renewed, q, w_raw, packed, table, bias, x_own, x_all, w_all, k_near, v_near, k_send, v_send, k_all, v_all,
    mixed, top, total, projected, squares, part_send, part_recv, norm_send, norm_recv, fresh, result,
    local_sem, out_sem, kv1_send, kv1_recv, kv2_send, kv2_recv,
    own_send, own_recv, other_send, other_recv, side_send, side_recv, flow_send, flow_recv,
    lend_send, lend_recv, core_send, core_recv, sum_send, sum_recv,
):
    store, head = lax.axis_index("store"), lax.axis_index("head")
    x, y, z, core = store // 4, store % 4, head // 2, head % 2

    def at_xy(dx, dy):
        return {"store": ((x + dx) % 4) * 4 + (y + dy) % 4, "head": head}

    def at_z(dz):
        return {"store": store, "head": ((z + dz) % 8) * 2 + core}

    sibling = {"store": store, "head": z * 2 + (1 - core)}

    half_of, odd = y // 2, y % 2
    source = z % 2 == half_of
    relay = z % 2 != half_of
    ally = {"store": x * 4 + y + 1 - 2 * odd, "head": head}
    partner = {"store": x * 4 + 3 - y, "head": head}
    x_mine = (z // 2) * 2 + core
    w_mine = x * 2 + odd

    loads = [
        pltpu.make_async_copy(kv_hbm.at[:, 0], k_near.at[x], local_sem.at[0]),
        pltpu.make_async_copy(kv_hbm.at[:, 1], v_near.at[y], local_sem.at[1]),
        pltpu.make_async_copy(w_hbm, w_raw, local_sem.at[3]),
        pltpu.make_async_copy(q_hbm, q, local_sem.at[4]),
        pltpu.make_async_copy(ids_hbm, ids, local_sem.at[5]),
        pltpu.make_async_copy(home_hbm, home, local_sem.at[6]),
        pltpu.make_async_copy(counts_hbm, counts, local_sem.at[7]),
        pltpu.make_async_copy(renewed_hbm, renewed, local_sem.at[8]),
    ]
    for load in loads:
        load.start()
    x_load = pltpu.make_async_copy(x_hbm, x_all.at[x_mine, pl.ds(0, ROWS)], local_sem.at[2])
    x_lent = pltpu.make_async_copy(x_hbm, x_own, local_sem.at[2])
    pl.when(source)(x_load.start)
    pl.when(relay)(x_lent.start)

    barrier = pltpu.get_barrier_semaphore()
    peers = [at_xy(d, 0) for d in (1, 3, 2)] + [at_xy(0, d) for d in (1, 3, 2)]
    peers += [at_z(1), at_z(7), sibling]
    for peer in peers:
        pl.semaphore_signal(barrier, inc=1, device_id=peer, device_id_type=MESH)
    pl.semaphore_wait(barrier, len(peers))

    def sems(ref, *lead):
        return lambda k: ref.at[(*lead, k)]

    def near_at(buf):
        return lambda i, part: buf.at[i] if part is None else buf.at[i, pl.ds(4 * part, 4)]

    def w_at(side, first, rows):
        def at(i, part):
            if part is None:
                return w_all.at[i * 2 + side, pl.ds(first, rows)]
            return w_all.at[i * 2 + side, pl.ds(first + part * (rows // 2), rows // 2)]

        return at

    along_x = (x, at_xy(1, 0), at_xy(3, 0))
    along_y = (y, at_xy(0, 1), at_xy(0, 3))
    k1 = Ring4(near_at(k_near), *along_x, sems(kv1_send, 0), sems(kv1_recv, 0))
    v1 = Ring4(near_at(v_near), *along_y, sems(kv1_send, 1), sems(kv1_recv, 1))
    own = Ring4(w_at(odd, 0, DEEP), *along_x, sems(own_send), sems(own_recv))
    other = Ring4(w_at(1 - odd, 0, DEEP // 2), *along_x, sems(other_send), sems(other_recv))

    def offset(j):
        return j + j // 2 - 2 * (j // 3)

    def side(j, sent=True):
        block = (x + offset(j % 4)) % 4 * 2 + (odd if sent else 1 - odd)
        piece = w_all.at[block, pl.ds(0 if j == 4 else DEEP // 2, DEEP // 2)]
        return remote(piece, piece, side_send.at[j], side_recv.at[j], ally)

    def x_piece(way, dist, w):
        at = (z + (8 - dist if way == 0 else dist)) % 8
        return x_all.at[(at // 2) * 2 + core, pl.ds(256 * w, 256)]

    def flow(way, stage, dist, w):
        piece = x_piece(way, dist, w)
        device = at_z(1 if way == 0 else 7)
        return remote(piece, piece, flow_send.at[way, stage, w], flow_recv.at[way, stage, w], device)

    def lend(half):
        return remote(
            x_own.at[pl.ds(256 * half, 256)], x_all.at[x_mine, pl.ds(ROWS + 256 * half, 256)],
            lend_send.at[half], lend_recv.at[half], partner,
        )

    def to_core(dist, part, mine=True):
        at = (z + 8 + dist) % 8
        piece = x_all.at[(at // 2) * 2 + (core if mine else 1 - core), pl.ds(ROWS * part, ROWS)]
        return remote(piece, piece, core_send.at[at // 2, part], core_recv.at[at // 2, part], sibling)

    def x_start():
        @pl.when(source)
        def _():
            x_load.wait()
            for w in (0, 1):
                flow(0, 0, 0, w).start()
                flow(1, 0, 0, w).start()
            to_core(0, 0).start()

        @pl.when(relay)
        def _():
            x_lent.wait()
            lend(0).start()
            lend(1).start()

    def x_one():
        @pl.when(relay)
        def _():
            for w in (0, 1):
                for way in (0, 1):
                    flow(way, 0, 1, w).wait_recv()
                    flow(way, 0, 1, w).start()
            to_core(-1, 0).start()
            to_core(1, 0).start()

        @pl.when(source)
        def _():
            for w in (2, 3):
                lend(w - 2).wait_recv()
                flow(0, 0, 0, w).start()
                flow(1, 0, 0, w).start()
            to_core(0, 1).start()

    def x_two(half):
        w = 2 + half

        @pl.when(relay)
        def _():
            for way in (0, 1):
                flow(way, 0, 1, w).wait_recv()
                flow(way, 0, 1, w).start()
            if half:
                to_core(-1, 1).start()
                to_core(1, 1).start()

        @pl.when(source)
        def _():
            for way in (0, 1):
                flow(way, 0, 2, half).wait_recv()
            if half:
                to_core(-2, 0).start()
                to_core(2, 0).start()

    def x_three(half):
        w = 2 + half

        @pl.when(source)
        def _():
            for way in (0, 1):
                flow(way, 0, 2, w).wait_recv()
                flow(way, 1, 2, w).start()
            if half:
                for way in (0, 1):
                    flow(way, 1, 2, 0).start()
                    flow(way, 1, 2, 1).start()
                to_core(-2, 1).start()
                to_core(2, 1).start()

    def x_relayed(part):
        @pl.when(relay)
        def _():
            for half in (0, 1):
                w = 2 * part + half
                for way in (0, 1):
                    flow(way, 1, 3, w).wait_recv()
                    if way == half:
                        flow(way, 1, 3, w).start()
            to_core(-3, part).start()
            to_core(3, part).start()

    def x_ended(part):
        @pl.when(source)
        def _():
            for way in (0, 1):
                flow(way, 1, 4, 2 * part + way).wait_recv()
            to_core(4, part).start()

    def x_others(part):
        for at in range(4):
            piece = x_all.at[at * 2 + 1 - core, pl.ds(ROWS * part, ROWS)]
            remote(piece, piece, core_send.at[at, part], core_recv.at[at, part], sibling).wait_recv()

    def x_drain():
        @pl.when(source)
        def _():
            for way in (0, 1):
                for w in range(4):
                    flow(way, 0, 0, w).wait_send()
                    flow(way, 1, 2, w).wait_send()

        @pl.when(relay)
        def _():
            lend(0).wait_send()
            lend(1).wait_send()
            for way in (0, 1):
                for w in range(4):
                    flow(way, 0, 1, w).wait_send()
                for part in (0, 1):
                    flow(way, 1, 3, 2 * part + way).wait_send()

        for at in range(4):
            for part in (0, 1):
                piece = x_all.at[at * 2 + core, pl.ds(ROWS * part, ROWS)]
                remote(piece, piece, core_send.at[at, part], core_recv.at[at, part], sibling).wait_send()

    def swap(half):
        rows = pl.ds(256 * half, 256)
        return remote(
            part_send.at[rows], part_recv.at[rows], sum_send.at[half], sum_recv.at[half], partner
        )

    swap_norm = remote(norm_send, norm_recv, sum_send.at[2], sum_recv.at[2], partner)

    def k2(r, d):
        return remote(
            k_send.at[(y + d) % 4, r], k_all.at[r, y],
            kv2_send.at[0, r, d - 1], kv2_recv.at[0, r, d - 1], at_xy(0, d),
        )

    def k2_arrived(r, d):
        remote(
            k_send.at[0, r], k_all.at[r, (y + 4 - d) % 4],
            kv2_send.at[0, r, d - 1], kv2_recv.at[0, r, d - 1], at_xy(0, d),
        ).wait_recv()

    def v2(r, d):
        return remote(
            v_send.at[(x + d) % 4, r], v_all.at[r, :, x],
            kv2_send.at[1, r, d - 1], kv2_recv.at[1, r, d - 1], at_xy(d, 0),
        )

    def v2_arrived(r, d):
        remote(
            v_send.at[0, r], v_all.at[r, :, (x + 4 - d) % 4],
            kv2_send.at[1, r, d - 1], kv2_recv.at[1, r, d - 1], at_xy(d, 0),
        ).wait_recv()

    def name_rows():
        named = ids[...]
        stored = lax.fori_loop(
            0, 128, lambda p, rows: jnp.where(named == p, home[p], rows), named, unroll=8
        )
        device = lax.broadcasted_iota(jnp.int32, (SLOTS, 64), 0)
        filled = jnp.zeros((SLOTS, 64), jnp.int32)
        for j in range(SLOTS):
            row = stored[j : j + 1, :]
            filled = jnp.where(device == (row >> 3), j * 8 + (row & 7), filled)
        packed[...] = jnp.zeros_like(packed)
        packed[:, pl.ds(0, 64)] = filled
        move = pltpu.make_async_copy(packed, table, local_sem.at[9])
        move.start()
        move.wait()

    def mask_positions():
        lane = lax.broadcasted_iota(jnp.int32, (1, SPAN), 1)
        block, inner = lane >> 6, lane & 63
        for r in range(REQS):
            mine = store * REQS + r
            place = jnp.zeros((1, SPAN), jnp.int32)
            for b in range(SLOTS):
                slot = table[(b % 4) * 4 + b // 4, mine] // 8
                place = jnp.where(block == b, slot * BLK, place)
            place = place + inner
            shift = jnp.where(place < counts[mine] * BLK, 0.0, MASKED)
            bias[r] = lax.fori_loop(
                0, SEL, lambda i, kept: jnp.where(place == renewed[r, i], MASKED, kept), shift, unroll=8
            )

    def send_keys(first, count):
        @pl.loop(first, first + count)
        def _(r):
            for yd in range(4):
                for xs in range(4):
                    row = table[xs * 4 + y, (x * 4 + yd) * REQS + r] % 8
                    k_send[yd, r, xs] = k_near[xs, row]
            k_all[r, y] = k_send[y, r]
            for d in (1, 3, 2):
                k2(r, d).start()

    def send_values(first, count):
        @pl.loop(first, first + count)
        def _(r):
            for xd in range(4):
                for ys in range(4):
                    row = table[x * 4 + ys, (xd * 4 + y) * REQS + r] % 8
                    v_send[xd, r, ys] = v_near[ys, row]
            for ys in range(4):
                v_all[r, ys, x] = v_send[x, r, ys]
            for d in (1, 3, 2):
                v2(r, d).start()

    def attend_cached(r):
        for d in (1, 3, 2):
            k2_arrived(r, d)
            v2_arrived(r, d)

        @pl.loop(0, QLEN // QTILE)
        def _(t):
            first = pl.multiple_of(t * QTILE, QTILE)
            shift = bias[r]
            for h in (0, 1):
                lanes = pl.ds(h * HD, HD)
                keys = k_all[r, :, :, :, lanes].reshape(SPAN, HD)
                values = v_all[r, :, :, :, lanes].reshape(SPAN, HD)
                scores = dot(q[r, pl.ds(first, QTILE), lanes], keys, NT) * TO_BASE_TWO + shift
                largest = jnp.max(scores, axis=-1, keepdims=True)
                exps = jnp.exp2(scores - largest)
                summed = jnp.sum(exps, axis=-1, keepdims=True)
                mixed[r, pl.ds(first, QTILE), lanes] = dot(exps.astype(jnp.bfloat16), values, NN)
                top[r, pl.ds(first, QTILE), lanes] = jnp.broadcast_to(largest, (QTILE, HD))
                total[r, pl.ds(first, QTILE), lanes] = jnp.broadcast_to(summed, (QTILE, HD))

    def project(part, half):
        rows = pl.ds(ROWS * part + 256 * half, 256)
        summed = dot(x_all[0, rows, :], w_all[0], NN)
        for b in range(1, 8):
            summed = summed + dot(x_all[b, rows, :], w_all[b], NN)
        return summed

    def sum_squares(part):
        squares[...] = jnp.zeros_like(squares)

        @pl.loop(0, 8)
        def _(b):
            wide = x_all[b, pl.ds(ROWS * part, ROWS), :].astype(jnp.float32)
            wide = wide * wide
            squares[...] += (wide[:, 0:128] + wide[:, 128:256]) + (wide[:, 256:384] + wide[:, 384:512])

    x_start()
    loads[0].wait()
    k1.start()
    loads[1].wait()
    v1.start()
    loads[2].wait()
    w_all[w_mine, :, pl.ds(0, FEAT)] = w_raw[:, 0, :]
    w_all[w_mine, :, pl.ds(FEAT, FEAT)] = w_raw[:, 1, :]
    side(4).start()
    loads[4].wait()
    loads[5].wait()
    name_rows()
    k1.forward()
    own.start()
    side(0).start()
    k1.finish()
    send_keys(0, 1)
    x_one()
    v1.forward()
    side(4, False).wait_recv()
    other.start()
    x_two(0)
    own.forward()
    side(1).start()
    side(2).start()
    x_two(1)
    v1.finish()
    send_values(0, 1)
    send_keys(1, 1)
    send_values(1, 1)
    x_three(0)
    loads[3].wait()
    loads[6].wait()
    loads[7].wait()
    mask_positions()
    other.forward()
    x_three(1)
    own.finish()
    side(3).start()
    send_keys(2, 2)
    send_values(2, 2)
    x_relayed(1)
    attend_cached(0)
    attend_cached(1)
    x_relayed(0)
    x_ended(1)
    other.finish()
    for j in range(4):
        side(j, False).wait_recv()
    x_others(1)

    for half in (0, 1):
        part_send[pl.ds(256 * half, 256), :] = project(1, half).astype(jnp.bfloat16)
        swap(half).start()
    x_ended(0)
    sum_squares(1)
    turned = jnp.transpose(squares[...])
    norm_send[...] = jnp.broadcast_to(jnp.sum(turned, axis=0, keepdims=True), norm_send.shape)
    swap_norm.start()
    x_others(0)
    sum_squares(0)
    for half in (0, 1):
        projected[pl.ds(256 * half, 256), :] = project(0, half)
    attend_cached(2)

    for half in (0, 1):
        swap(half).wait_recv()
    swap_norm.wait_recv()
    lent = jnp.transpose(jnp.broadcast_to(norm_recv[0:1, :], (HD, ROWS)))
    mean = (jnp.sum(squares[...], axis=-1, keepdims=True) + lent) * (1.0 / D)
    scale = lax.rsqrt(mean + EPS)
    for i in range(4):
        lanes = pl.ds(i * HD, HD)
        summed = projected[:, lanes] + part_recv[:, lanes].astype(jnp.float32)
        at = i * HD if i < 2 else FEAT + (i - 2) * 2 * HD
        fresh[:, pl.ds(at, HD)] = (summed * scale).astype(jnp.bfloat16)
        if i >= 2:
            fresh[:, pl.ds(at + HD, HD)] = jnp.ones((ROWS, HD), jnp.bfloat16)

    def store_result(r):
        return pltpu.make_async_copy(result.at[r], out_hbm.at[r], out_sem.at[r])

    @pl.loop(0, 3)
    def _(r):
        rows = pl.ds(pl.multiple_of(r * SEL, SEL), SEL)
        for h in (0, 1):
            lanes = pl.ds(h * HD, HD)
            scores = dot(q[r, :, lanes], fresh[rows, lanes], NT) * TO_BASE_TWO
            before = top[r, :, lanes]
            largest = jnp.maximum(before, jnp.max(scores, axis=-1, keepdims=True))
            exps = jnp.exp2(scores - largest)
            fade = jnp.exp2(before - largest)
            both = dot(exps.astype(jnp.bfloat16), fresh[rows, pl.ds(FEAT + h * 2 * HD, 2 * HD)], NN)
            attended = (mixed[r, :, lanes] * fade + both[:, 0:HD]) / (total[r, :, lanes] * fade + both[:, HD:])
            result[r, :, lanes] = attended.astype(jnp.bfloat16)
        store_result(r).start()

    r = REQS - 1
    for d in (1, 3, 2):
        k2_arrived(r, d)
        v2_arrived(r, d)

    @pl.loop(0, QLEN // QTILE)
    def _(t):
        rows = pl.ds(pl.multiple_of(t * QTILE, QTILE), QTILE)
        shift = bias[r]
        for h in (0, 1):
            lanes = pl.ds(h * HD, HD)
            tail = pl.ds(r * SEL, SEL)
            keys = k_all[r, :, :, :, lanes].reshape(SPAN, HD)
            values = v_all[r, :, :, :, lanes].reshape(SPAN, HD)
            scores = dot(q[r, rows, lanes], keys, NT) * TO_BASE_TWO + shift
            extra = dot(q[r, rows, lanes], fresh[tail, lanes], NT) * TO_BASE_TWO
            largest = jnp.maximum(
                jnp.max(scores, axis=-1, keepdims=True), jnp.max(extra, axis=-1, keepdims=True)
            )
            exps = jnp.exp2(scores - largest)
            more = jnp.exp2(extra - largest)
            summed = jnp.sum(exps, axis=-1, keepdims=True) + jnp.sum(more, axis=-1, keepdims=True)
            blend = dot(exps.astype(jnp.bfloat16), values, NN) + dot(
                more.astype(jnp.bfloat16), fresh[tail, pl.ds(FEAT + h * 2 * HD, HD)], NN
            )
            result[r, rows, lanes] = (blend / summed).astype(jnp.bfloat16)

    store_result(r).start()

    for ring in (k1, v1, own, other):
        ring.drain()
    for j in range(5):
        side(j).wait_send()

    @pl.loop(0, REQS)
    def _(r):
        for d in (1, 2, 3):
            k2(r, d).wait_send()
            v2(r, d).wait_send()

    x_drain()
    swap(0).wait_send()
    swap(1).wait_send()
    swap_norm.wait_send()
    for r in range(REQS):
        store_result(r).wait()


def attend(q, kv, rows, weights, ids, home, counts, renewed):
    hbm = pl.BlockSpec(memory_space=pltpu.HBM)
    bf, f32 = jnp.bfloat16, jnp.float32
    dma = pltpu.SemaphoreType.DMA
    return pl.pallas_call(
        kernel,
        out_shape=jax.ShapeDtypeStruct((REQS, QLEN, FEAT), bf),
        in_specs=[hbm] * 8,
        out_specs=pl.BlockSpec(memory_space=pl.ANY),
        scratch_shapes=[
            pltpu.VMEM((SLOTS, 64), jnp.int32),
            pltpu.SMEM((128,), jnp.int32),
            pltpu.SMEM((64,), jnp.int32),
            pltpu.SMEM((REQS, SEL), jnp.int32),
            pltpu.VMEM((REQS, QLEN, FEAT), bf),
            pltpu.VMEM((DEEP, 2, FEAT), bf),
            pltpu.VMEM((SLOTS, 128), jnp.int32),
            pltpu.SMEM((SLOTS, 128), jnp.int32),
            pltpu.VMEM((REQS, 1, SPAN), f32),
            pltpu.VMEM((ROWS, DEEP), bf),
            pltpu.VMEM((8, 2 * ROWS, DEEP), bf),
            pltpu.VMEM((8, DEEP, 2 * FEAT), bf),
            pltpu.VMEM((4, 8, BLK, FEAT), bf),
            pltpu.VMEM((4, 8, BLK, FEAT), bf),
            pltpu.VMEM((4, REQS, 4, BLK, FEAT), bf),
            pltpu.VMEM((4, REQS, 4, BLK, FEAT), bf),
            pltpu.VMEM((REQS, 4, 4, BLK, FEAT), bf),
            pltpu.VMEM((REQS, 4, 4, BLK, FEAT), bf),
            pltpu.VMEM((REQS, QLEN, FEAT), f32),
            pltpu.VMEM((REQS, QLEN, FEAT), f32),
            pltpu.VMEM((REQS, QLEN, FEAT), f32),
            pltpu.VMEM((ROWS, 2 * FEAT), f32),
            pltpu.VMEM((ROWS, HD), f32),
            pltpu.VMEM((ROWS, 2 * FEAT), bf),
            pltpu.VMEM((ROWS, 2 * FEAT), bf),
            pltpu.VMEM((8, ROWS), f32),
            pltpu.VMEM((8, ROWS), f32),
            pltpu.VMEM((ROWS, 3 * FEAT), bf),
            pltpu.VMEM((REQS, QLEN, FEAT), bf),
            dma((11,)),
            dma((REQS,)),
            dma((2, 4)), dma((2, 4)),
            dma((2, REQS, 3)), dma((2, REQS, 3)),
            dma((4,)), dma((4,)),
            dma((4,)), dma((4,)),
            dma((5,)), dma((5,)),
            dma((2, 2, 4)), dma((2, 2, 4)),
            dma((2,)), dma((2,)),
            dma((4, 2)), dma((4, 2)),
            dma((3,)), dma((3,)),
        ],
        compiler_params=pltpu.CompilerParams(
            collective_id=0, has_side_effects=True, vmem_limit_bytes=60 * 1024 * 1024
        ),
        cost_estimate=pl.CostEstimate(
            flops=14_000_000_000, bytes_accessed=8_000_000, transcendentals=10_000_000
        ),
        name="blend",
    )(q, kv, rows, weights, ids, home, counts, renewed)


def local(
    queries, kv_store, hidden_rows, w_kv, passage_ids, passage_home, passage_counts, recompute_pos
):
    return attend(
        queries,
        kv_store,
        hidden_rows.reshape(ROWS, DEEP),
        w_kv,
        passage_ids.T,
        passage_home,
        passage_counts,
        recompute_pos,
    )


def solution(mesh):
    placed = (
        P("store", None, "head"),
        P("store", None, None, "head"),
        P("store", None, "head"),
        P("store", None, "head"),
        P(),
        P(),
        P(),
        P("store", None),
    )
    return jax.shard_map(
        local, mesh=mesh, in_specs=placed, out_specs=P("store", None, "head"), check_vma=False
    )
```

```python
import math

import jax
import jax.numpy as jnp
from jax import lax
from jax.experimental import pallas as pl
from jax.experimental.pallas import tpu as pltpu
from jax.sharding import PartitionSpec as P

MESH = pl.DeviceIdType.MESH

D = 8192
HD = 128
EPS = 1e-06
SLOTS = 16
BLK = 64
SPAN = SLOTS * BLK
REQS = 4
QLEN = 1024
SEL = 128
FEAT = 256
ROWS = REQS * SEL
DEEP = 512
QTILE = 512
MASKED = -1e28
TO_BASE_TWO = HD ** (-0.5) * math.log2(math.e)

NT = (((1,), (1,)), ((), ()))
NN = (((1,), (0,)), ((), ()))


def dot(a, b, dims):
    return lax.dot_general(a, b, dims, preferred_element_type=jnp.float32)


def remote(src, dst, send_sem, recv_sem, device):
    return pltpu.make_async_remote_copy(
        src_ref=src,
        dst_ref=dst,
        send_sem=send_sem,
        recv_sem=recv_sem,
        device_id=device,
        device_id_type=MESH,
    )


class Ring4:
    def __init__(self, at, me, plus, minus, send, recv):
        self.at, self.plus, self.minus, self.send, self.recv = at, plus, minus, send, recv
        self.me, self.prev, self.next, self.far = me, (me + 3) % 4, (me + 1) % 4, (me + 2) % 4

    def copy(self, source, part, k, device):
        piece = self.at(source, part)
        return remote(piece, piece, self.send(k), self.recv(k), device)

    def start(self):
        self.copy(self.me, None, 0, self.plus).start()
        self.copy(self.me, None, 1, self.minus).start()

    def forward(self):
        self.copy(self.prev, None, 0, self.plus).wait_recv()
        self.copy(self.prev, 0, 2, self.plus).start()
        self.copy(self.next, None, 1, self.minus).wait_recv()
        self.copy(self.next, 1, 3, self.minus).start()

    def finish(self):
        self.copy(self.far, 0, 2, self.plus).wait_recv()
        self.copy(self.far, 1, 3, self.minus).wait_recv()

    def drain(self):
        self.copy(self.me, None, 0, self.plus).wait_send()
        self.copy(self.me, None, 1, self.minus).wait_send()
        self.copy(self.prev, 0, 2, self.plus).wait_send()
        self.copy(self.next, 1, 3, self.minus).wait_send()


def kernel(
    q_hbm, kv_hbm, x_hbm, w_hbm, ids_hbm, home_hbm, counts_hbm, renewed_hbm, out_hbm,
    ids, home, counts, renewed, q, w_raw, packed, table, bias, x_own, x_all, w_all, k_near, v_near, k_send, v_send, k_all, v_all,
    mixed, top, total, projected, squares, part_send, part_recv, norm_send, norm_recv, fresh, result,
    local_sem, out_sem, kv1_send, kv1_recv, kv2_send, kv2_recv,
    own_send, own_recv, other_send, other_recv, side_send, side_recv, flow_send, flow_recv,
    lend_send, lend_recv, core_send, core_recv, sum_send, sum_recv,
):
    store, head = lax.axis_index("store"), lax.axis_index("head")
    x, y, z, core = store // 4, store % 4, head // 2, head % 2

    def at_xy(dx, dy):
        return {"store": ((x + dx) % 4) * 4 + (y + dy) % 4, "head": head}

    def at_z(dz):
        return {"store": store, "head": ((z + dz) % 8) * 2 + core}

    sibling = {"store": store, "head": z * 2 + (1 - core)}

    half_of, odd = y // 2, y % 2
    source = z % 2 == half_of
    relay = z % 2 != half_of
    ally = {"store": x * 4 + y + 1 - 2 * odd, "head": head}
    partner = {"store": x * 4 + 3 - y, "head": head}
    x_mine = (z // 2) * 2 + core
    w_mine = x * 2 + odd

    loads = [
        pltpu.make_async_copy(kv_hbm.at[:, 0], k_near.at[x], local_sem.at[0]),
        pltpu.make_async_copy(kv_hbm.at[:, 1], v_near.at[y], local_sem.at[1]),
        pltpu.make_async_copy(w_hbm, w_raw, local_sem.at[3]),
        pltpu.make_async_copy(q_hbm, q, local_sem.at[4]),
        pltpu.make_async_copy(ids_hbm, ids, local_sem.at[5]),
        pltpu.make_async_copy(home_hbm, home, local_sem.at[6]),
        pltpu.make_async_copy(counts_hbm, counts, local_sem.at[7]),
        pltpu.make_async_copy(renewed_hbm, renewed, local_sem.at[8]),
    ]
    for load in loads:
        load.start()
    x_load = pltpu.make_async_copy(x_hbm, x_all.at[x_mine, pl.ds(0, ROWS)], local_sem.at[2])
    x_lent = pltpu.make_async_copy(x_hbm, x_own, local_sem.at[2])
    pl.when(source)(x_load.start)
    pl.when(relay)(x_lent.start)

    barrier = pltpu.get_barrier_semaphore()
    peers = [at_xy(d, 0) for d in (1, 3, 2)] + [at_xy(0, d) for d in (1, 3, 2)]
    peers += [at_z(1), at_z(7), sibling]
    for peer in peers:
        pl.semaphore_signal(barrier, inc=1, device_id=peer, device_id_type=MESH)
    pl.semaphore_wait(barrier, len(peers))

    def sems(ref, *lead):
        return lambda k: ref.at[(*lead, k)]

    def near_at(buf):
        return lambda i, part: buf.at[i] if part is None else buf.at[i, pl.ds(4 * part, 4)]

    def w_at(side, first, rows):
        def at(i, part):
            if part is None:
                return w_all.at[i * 2 + side, pl.ds(first, rows)]
            return w_all.at[i * 2 + side, pl.ds(first + part * (rows // 2), rows // 2)]

        return at

    along_x = (x, at_xy(1, 0), at_xy(3, 0))
    along_y = (y, at_xy(0, 1), at_xy(0, 3))
    k1 = Ring4(near_at(k_near), *along_x, sems(kv1_send, 0), sems(kv1_recv, 0))
    v1 = Ring4(near_at(v_near), *along_y, sems(kv1_send, 1), sems(kv1_recv, 1))
    own = Ring4(w_at(odd, 0, DEEP), *along_x, sems(own_send), sems(own_recv))
    other = Ring4(w_at(1 - odd, 0, DEEP // 2), *along_x, sems(other_send), sems(other_recv))

    def offset(j):
        return j + j // 2 - 2 * (j // 3)

    def side(j, sent=True):
        block = (x + offset(j % 4)) % 4 * 2 + (odd if sent else 1 - odd)
        piece = w_all.at[block, pl.ds(0 if j == 4 else DEEP // 2, DEEP // 2)]
        return remote(piece, piece, side_send.at[j], side_recv.at[j], ally)

    def x_piece(way, dist, w):
        at = (z + (8 - dist if way == 0 else dist)) % 8
        return x_all.at[(at // 2) * 2 + core, pl.ds(256 * w, 256)]

    def flow(way, stage, dist, w):
        piece = x_piece(way, dist, w)
        device = at_z(1 if way == 0 else 7)
        return remote(piece, piece, flow_send.at[way, stage, w], flow_recv.at[way, stage, w], device)

    def lend(half):
        return remote(
            x_own.at[pl.ds(256 * half, 256)], x_all.at[x_mine, pl.ds(ROWS + 256 * half, 256)],
            lend_send.at[half], lend_recv.at[half], partner,
        )

    def to_core(dist, *pieces):
        at = (z + 8 + dist) % 8
        for w in pieces:
            piece = x_all.at[(at // 2) * 2 + core, pl.ds(256 * w, 256)]
            remote(piece, piece, core_send.at[at // 2, w], core_recv.at[at // 2, w], sibling).start()

    def x_start():
        @pl.when(source)
        def _():
            x_load.wait()
            for w in (0, 1):
                flow(0, 0, 0, w).start()
                flow(1, 0, 0, w).start()
            to_core(0, 0, 1)

        @pl.when(relay)
        def _():
            x_lent.wait()
            lend(0).start()
            lend(1).start()

    def x_one():
        @pl.when(relay)
        def _():
            for w in (0, 1):
                for way in (0, 1):
                    flow(way, 0, 1, w).wait_recv()
                    flow(way, 0, 1, w).start()
            to_core(-1, 0, 1)
            to_core(1, 0, 1)

        @pl.when(source)
        def _():
            for w in (2, 3):
                lend(w - 2).wait_recv()
                flow(0, 0, 0, w).start()
                flow(1, 0, 0, w).start()
            to_core(0, 2, 3)

    def x_two(half):
        w = 2 + half

        @pl.when(relay)
        def _():
            for way in (0, 1):
                flow(way, 0, 1, w).wait_recv()
                flow(way, 0, 1, w).start()
            if half:
                to_core(-1, 2, 3)
                to_core(1, 2, 3)

        @pl.when(source)
        def _():
            for way in (0, 1):
                flow(way, 0, 2, half).wait_recv()
            if half:
                to_core(-2, 0, 1)
                to_core(2, 0, 1)

    def x_three(half):
        w = 2 + half

        @pl.when(source)
        def _():
            for way in (0, 1):
                flow(way, 0, 2, w).wait_recv()
                flow(way, 1, 2, w).start()
            if half:
                for way in (0, 1):
                    flow(way, 1, 2, 0).start()
                    flow(way, 1, 2, 1).start()
                to_core(-2, 2, 3)
                to_core(2, 2, 3)

    def x_relayed(part):
        @pl.when(relay)
        def _():
            for half in (0, 1):
                w = 2 * part + half
                for way in (0, 1):
                    flow(way, 1, 3, w).wait_recv()
                    if way == half:
                        flow(way, 1, 3, w).start()
                to_core(-3, w)
                to_core(3, w)

    def x_ended(w):
        @pl.when(source)
        def _():
            flow(w % 2, 1, 4, w).wait_recv()
            to_core(4, w)

    def x_others(w):
        for at in range(4):
            piece = x_all.at[at * 2 + 1 - core, pl.ds(256 * w, 256)]
            remote(piece, piece, core_send.at[at, w], core_recv.at[at, w], sibling).wait_recv()

    def x_drain():
        @pl.when(source)
        def _():
            for way in (0, 1):
                for w in range(4):
                    flow(way, 0, 0, w).wait_send()
                    flow(way, 1, 2, w).wait_send()

        @pl.when(relay)
        def _():
            lend(0).wait_send()
            lend(1).wait_send()
            for way in (0, 1):
                for w in range(4):
                    flow(way, 0, 1, w).wait_send()
                for part in (0, 1):
                    flow(way, 1, 3, 2 * part + way).wait_send()

        for at in range(4):
            for w in range(4):
                piece = x_all.at[at * 2 + core, pl.ds(256 * w, 256)]
                remote(piece, piece, core_send.at[at, w], core_recv.at[at, w], sibling).wait_send()

    def swap(half):
        rows = pl.ds(256 * half, 256)
        return remote(
            part_send.at[rows], part_recv.at[rows], sum_send.at[half], sum_recv.at[half], partner
        )

    swap_norm = remote(norm_send, norm_recv, sum_send.at[2], sum_recv.at[2], partner)

    def k2(r, d):
        return remote(
            k_send.at[(y + d) % 4, r], k_all.at[r, y],
            kv2_send.at[0, r, d - 1], kv2_recv.at[0, r, d - 1], at_xy(0, d),
        )

    def k2_arrived(r, d):
        remote(
            k_send.at[0, r], k_all.at[r, (y + 4 - d) % 4],
            kv2_send.at[0, r, d - 1], kv2_recv.at[0, r, d - 1], at_xy(0, d),
        ).wait_recv()

    def v2(r, d):
        return remote(
            v_send.at[(x + d) % 4, r], v_all.at[r, :, x],
            kv2_send.at[1, r, d - 1], kv2_recv.at[1, r, d - 1], at_xy(d, 0),
        )

    def v2_arrived(r, d):
        remote(
            v_send.at[0, r], v_all.at[r, :, (x + 4 - d) % 4],
            kv2_send.at[1, r, d - 1], kv2_recv.at[1, r, d - 1], at_xy(d, 0),
        ).wait_recv()

    def name_rows():
        named = ids[...]
        stored = lax.fori_loop(
            0, 128, lambda p, rows: jnp.where(named == p, home[p], rows), named, unroll=8
        )
        device = lax.broadcasted_iota(jnp.int32, (SLOTS, 64), 0)
        filled = jnp.zeros((SLOTS, 64), jnp.int32)
        for j in range(SLOTS):
            row = stored[j : j + 1, :]
            filled = jnp.where(device == (row >> 3), j * 8 + (row & 7), filled)
        packed[...] = jnp.zeros_like(packed)
        packed[:, pl.ds(0, 64)] = filled
        move = pltpu.make_async_copy(packed, table, local_sem.at[9])
        move.start()
        move.wait()

    def mask_positions():
        lane = lax.broadcasted_iota(jnp.int32, (1, SPAN), 1)
        block, inner = lane >> 6, lane & 63
        for r in range(REQS):
            mine = store * REQS + r
            place = jnp.zeros((1, SPAN), jnp.int32)
            for b in range(SLOTS):
                slot = table[(b % 4) * 4 + b // 4, mine] // 8
                place = jnp.where(block == b, slot * BLK, place)
            place = place + inner
            shift = jnp.where(place < counts[mine] * BLK, 0.0, MASKED)
            bias[r] = lax.fori_loop(
                0, SEL, lambda i, kept: jnp.where(place == renewed[r, i], MASKED, kept), shift, unroll=8
            )

    def send_keys(first, count):
        @pl.loop(first, first + count)
        def _(r):
            for yd in range(4):
                for xs in range(4):
                    row = table[xs * 4 + y, (x * 4 + yd) * REQS + r] % 8
                    k_send[yd, r, xs] = k_near[xs, row]
            k_all[r, y] = k_send[y, r]
            for d in (1, 3, 2):
                k2(r, d).start()

    def send_values(first, count):
        @pl.loop(first, first + count)
        def _(r):
            for xd in range(4):
                for ys in range(4):
                    row = table[x * 4 + ys, (xd * 4 + y) * REQS + r] % 8
                    v_send[xd, r, ys] = v_near[ys, row]
            for ys in range(4):
                v_all[r, ys, x] = v_send[x, r, ys]
            for d in (1, 3, 2):
                v2(r, d).start()

    def attend_cached(r):
        for d in (1, 3, 2):
            k2_arrived(r, d)
            v2_arrived(r, d)

        @pl.loop(0, QLEN // QTILE)
        def _(t):
            first = pl.multiple_of(t * QTILE, QTILE)
            shift = bias[r]
            for h in (0, 1):
                lanes = pl.ds(h * HD, HD)
                keys = k_all[r, :, :, :, lanes].reshape(SPAN, HD)
                values = v_all[r, :, :, :, lanes].reshape(SPAN, HD)
                scores = dot(q[r, pl.ds(first, QTILE), lanes], keys, NT) * TO_BASE_TWO + shift
                largest = jnp.max(scores, axis=-1, keepdims=True)
                exps = jnp.exp2(scores - largest)
                summed = jnp.sum(exps, axis=-1, keepdims=True)
                mixed[r, pl.ds(first, QTILE), lanes] = dot(exps.astype(jnp.bfloat16), values, NN)
                top[r, pl.ds(first, QTILE), lanes] = jnp.broadcast_to(largest, (QTILE, HD))
                total[r, pl.ds(first, QTILE), lanes] = jnp.broadcast_to(summed, (QTILE, HD))

    def project(part, half):
        rows = pl.ds(ROWS * part + 256 * half, 256)
        summed = dot(x_all[0, rows, :], w_all[0], NN)
        for b in range(1, 8):
            summed = summed + dot(x_all[b, rows, :], w_all[b], NN)
        return summed

    def sum_squares(part):
        squares[...] = jnp.zeros_like(squares)

        @pl.loop(0, 8)
        def _(b):
            wide = x_all[b, pl.ds(ROWS * part, ROWS), :].astype(jnp.float32)
            wide = wide * wide
            squares[...] += (wide[:, 0:128] + wide[:, 128:256]) + (wide[:, 256:384] + wide[:, 384:512])

    x_start()
    loads[0].wait()
    k1.start()
    loads[1].wait()
    v1.start()
    loads[2].wait()
    w_all[w_mine, :, pl.ds(0, FEAT)] = w_raw[:, 0, :]
    w_all[w_mine, :, pl.ds(FEAT, FEAT)] = w_raw[:, 1, :]
    side(4).start()
    loads[4].wait()
    loads[5].wait()
    name_rows()
    k1.forward()
    own.start()
    side(0).start()
    k1.finish()
    send_keys(0, 1)
    x_one()
    v1.forward()
    side(4, False).wait_recv()
    other.start()
    x_two(0)
    own.forward()
    side(1).start()
    side(2).start()
    x_two(1)
    v1.finish()
    send_values(0, 1)
    x_three(0)
    loads[3].wait()
    loads[6].wait()
    loads[7].wait()
    mask_positions()
    other.forward()
    x_three(1)
    own.finish()
    side(3).start()
    send_keys(1, 3)
    send_values(1, 3)
    x_relayed(1)
    attend_cached(0)
    x_ended(2)
    other.finish()
    for j in range(4):
        side(j, False).wait_recv()
    x_others(2)
    part_send[pl.ds(0, 256), :] = project(1, 0).astype(jnp.bfloat16)
    swap(0).start()
    x_ended(3)
    x_others(3)
    part_send[pl.ds(256, 256), :] = project(1, 1).astype(jnp.bfloat16)
    swap(1).start()
    x_relayed(0)
    sum_squares(1)
    turned = jnp.transpose(squares[...])
    norm_send[...] = jnp.broadcast_to(jnp.sum(turned, axis=0, keepdims=True), norm_send.shape)
    swap_norm.start()
    attend_cached(1)
    x_ended(0)
    x_ended(1)
    x_others(0)
    x_others(1)
    sum_squares(0)
    for half in (0, 1):
        projected[pl.ds(256 * half, 256), :] = project(0, half)
    attend_cached(2)

    for half in (0, 1):
        swap(half).wait_recv()
    swap_norm.wait_recv()
    lent = jnp.transpose(jnp.broadcast_to(norm_recv[0:1, :], (HD, ROWS)))
    mean = (jnp.sum(squares[...], axis=-1, keepdims=True) + lent) * (1.0 / D)
    scale = lax.rsqrt(mean + EPS)
    for i in range(4):
        lanes = pl.ds(i * HD, HD)
        summed = projected[:, lanes] + part_recv[:, lanes].astype(jnp.float32)
        at = i * HD if i < 2 else FEAT + (i - 2) * 2 * HD
        fresh[:, pl.ds(at, HD)] = (summed * scale).astype(jnp.bfloat16)
        if i >= 2:
            fresh[:, pl.ds(at + HD, HD)] = jnp.ones((ROWS, HD), jnp.bfloat16)

    def store_result(r):
        return pltpu.make_async_copy(result.at[r], out_hbm.at[r], out_sem.at[r])

    @pl.loop(0, 3)
    def _(r):
        rows = pl.ds(pl.multiple_of(r * SEL, SEL), SEL)
        for h in (0, 1):
            lanes = pl.ds(h * HD, HD)
            scores = dot(q[r, :, lanes], fresh[rows, lanes], NT) * TO_BASE_TWO
            before = top[r, :, lanes]
            largest = jnp.maximum(before, jnp.max(scores, axis=-1, keepdims=True))
            exps = jnp.exp2(scores - largest)
            fade = jnp.exp2(before - largest)
            both = dot(exps.astype(jnp.bfloat16), fresh[rows, pl.ds(FEAT + h * 2 * HD, 2 * HD)], NN)
            attended = (mixed[r, :, lanes] * fade + both[:, 0:HD]) / (total[r, :, lanes] * fade + both[:, HD:])
            result[r, :, lanes] = attended.astype(jnp.bfloat16)
        store_result(r).start()

    r = REQS - 1
    for d in (1, 3, 2):
        k2_arrived(r, d)
        v2_arrived(r, d)

    @pl.loop(0, QLEN // QTILE)
    def _(t):
        rows = pl.ds(pl.multiple_of(t * QTILE, QTILE), QTILE)
        shift = bias[r]
        for h in (0, 1):
            lanes = pl.ds(h * HD, HD)
            tail = pl.ds(r * SEL, SEL)
            keys = k_all[r, :, :, :, lanes].reshape(SPAN, HD)
            values = v_all[r, :, :, :, lanes].reshape(SPAN, HD)
            scores = dot(q[r, rows, lanes], keys, NT) * TO_BASE_TWO + shift
            extra = dot(q[r, rows, lanes], fresh[tail, lanes], NT) * TO_BASE_TWO
            largest = jnp.maximum(
                jnp.max(scores, axis=-1, keepdims=True), jnp.max(extra, axis=-1, keepdims=True)
            )
            exps = jnp.exp2(scores - largest)
            more = jnp.exp2(extra - largest)
            summed = jnp.sum(exps, axis=-1, keepdims=True) + jnp.sum(more, axis=-1, keepdims=True)
            blend = dot(exps.astype(jnp.bfloat16), values, NN) + dot(
                more.astype(jnp.bfloat16), fresh[tail, pl.ds(FEAT + h * 2 * HD, HD)], NN
            )
            result[r, rows, lanes] = (blend / summed).astype(jnp.bfloat16)

    store_result(r).start()

    for ring in (k1, v1, own, other):
        ring.drain()
    for j in range(5):
        side(j).wait_send()

    @pl.loop(0, REQS)
    def _(r):
        for d in (1, 2, 3):
            k2(r, d).wait_send()
            v2(r, d).wait_send()

    x_drain()
    swap(0).wait_send()
    swap(1).wait_send()
    swap_norm.wait_send()
    for r in range(REQS):
        store_result(r).wait()


def attend(q, kv, rows, weights, ids, home, counts, renewed):
    hbm = pl.BlockSpec(memory_space=pltpu.HBM)
    bf, f32 = jnp.bfloat16, jnp.float32
    dma = pltpu.SemaphoreType.DMA
    return pl.pallas_call(
        kernel,
        out_shape=jax.ShapeDtypeStruct((REQS, QLEN, FEAT), bf),
        in_specs=[hbm] * 8,
        out_specs=pl.BlockSpec(memory_space=pl.ANY),
        scratch_shapes=[
            pltpu.VMEM((SLOTS, 64), jnp.int32),
            pltpu.SMEM((128,), jnp.int32),
            pltpu.SMEM((64,), jnp.int32),
            pltpu.SMEM((REQS, SEL), jnp.int32),
            pltpu.VMEM((REQS, QLEN, FEAT), bf),
            pltpu.VMEM((DEEP, 2, FEAT), bf),
            pltpu.VMEM((SLOTS, 128), jnp.int32),
            pltpu.SMEM((SLOTS, 128), jnp.int32),
            pltpu.VMEM((REQS, 1, SPAN), f32),
            pltpu.VMEM((ROWS, DEEP), bf),
            pltpu.VMEM((8, 2 * ROWS, DEEP), bf),
            pltpu.VMEM((8, DEEP, 2 * FEAT), bf),
            pltpu.VMEM((4, 8, BLK, FEAT), bf),
            pltpu.VMEM((4, 8, BLK, FEAT), bf),
            pltpu.VMEM((4, REQS, 4, BLK, FEAT), bf),
            pltpu.VMEM((4, REQS, 4, BLK, FEAT), bf),
            pltpu.VMEM((REQS, 4, 4, BLK, FEAT), bf),
            pltpu.VMEM((REQS, 4, 4, BLK, FEAT), bf),
            pltpu.VMEM((REQS, QLEN, FEAT), f32),
            pltpu.VMEM((REQS, QLEN, FEAT), f32),
            pltpu.VMEM((REQS, QLEN, FEAT), f32),
            pltpu.VMEM((ROWS, 2 * FEAT), f32),
            pltpu.VMEM((ROWS, HD), f32),
            pltpu.VMEM((ROWS, 2 * FEAT), bf),
            pltpu.VMEM((ROWS, 2 * FEAT), bf),
            pltpu.VMEM((8, ROWS), f32),
            pltpu.VMEM((8, ROWS), f32),
            pltpu.VMEM((ROWS, 3 * FEAT), bf),
            pltpu.VMEM((REQS, QLEN, FEAT), bf),
            dma((11,)),
            dma((REQS,)),
            dma((2, 4)), dma((2, 4)),
            dma((2, REQS, 3)), dma((2, REQS, 3)),
            dma((4,)), dma((4,)),
            dma((4,)), dma((4,)),
            dma((5,)), dma((5,)),
            dma((2, 2, 4)), dma((2, 2, 4)),
            dma((2,)), dma((2,)),
            dma((4, 4)), dma((4, 4)),
            dma((3,)), dma((3,)),
        ],
        compiler_params=pltpu.CompilerParams(
            collective_id=0, has_side_effects=True, vmem_limit_bytes=60 * 1024 * 1024
        ),
        cost_estimate=pl.CostEstimate(
            flops=14_000_000_000, bytes_accessed=8_000_000, transcendentals=10_000_000
        ),
        name="blend",
    )(q, kv, rows, weights, ids, home, counts, renewed)


def local(
    queries, kv_store, hidden_rows, w_kv, passage_ids, passage_home, passage_counts, recompute_pos
):
    return attend(
        queries,
        kv_store,
        hidden_rows.reshape(ROWS, DEEP),
        w_kv,
        passage_ids.T,
        passage_home,
        passage_counts,
        recompute_pos,
    )


def solution(mesh):
    placed = (
        P("store", None, "head"),
        P("store", None, None, "head"),
        P("store", None, "head"),
        P("store", None, "head"),
        P(),
        P(),
        P(),
        P("store", None),
    )
    return jax.shard_map(
        local, mesh=mesh, in_specs=placed, out_specs=P("store", None, "head"), check_vma=False
    )
```

```python
import math

import jax
import jax.numpy as jnp
from jax import lax
from jax.experimental import pallas as pl
from jax.experimental.pallas import tpu as pltpu
from jax.sharding import PartitionSpec as P

MESH = pl.DeviceIdType.MESH

D = 8192
HD = 128
EPS = 1e-06
SLOTS = 16
BLK = 64
SPAN = SLOTS * BLK
REQS = 4
QLEN = 1024
SEL = 128
FEAT = 256
ROWS = REQS * SEL
DEEP = 512
QTILE = 512
MASKED = -1e28
TO_BASE_TWO = HD ** (-0.5) * math.log2(math.e)

NT = (((1,), (1,)), ((), ()))
NN = (((1,), (0,)), ((), ()))


def dot(a, b, dims):
    return lax.dot_general(a, b, dims, preferred_element_type=jnp.float32)


def remote(src, dst, send_sem, recv_sem, device):
    return pltpu.make_async_remote_copy(
        src_ref=src,
        dst_ref=dst,
        send_sem=send_sem,
        recv_sem=recv_sem,
        device_id=device,
        device_id_type=MESH,
    )


class Ring4:
    def __init__(self, at, me, plus, minus, send, recv):
        self.at, self.plus, self.minus, self.send, self.recv = at, plus, minus, send, recv
        self.me, self.prev, self.next, self.far = me, (me + 3) % 4, (me + 1) % 4, (me + 2) % 4

    def copy(self, source, part, k, device):
        piece = self.at(source, part)
        return remote(piece, piece, self.send(k), self.recv(k), device)

    def start(self):
        self.copy(self.me, None, 0, self.plus).start()
        self.copy(self.me, None, 1, self.minus).start()

    def forward(self):
        self.copy(self.prev, None, 0, self.plus).wait_recv()
        self.copy(self.prev, 0, 2, self.plus).start()
        self.copy(self.next, None, 1, self.minus).wait_recv()
        self.copy(self.next, 1, 3, self.minus).start()

    def finish(self):
        self.copy(self.far, 0, 2, self.plus).wait_recv()
        self.copy(self.far, 1, 3, self.minus).wait_recv()

    def drain(self):
        self.copy(self.me, None, 0, self.plus).wait_send()
        self.copy(self.me, None, 1, self.minus).wait_send()
        self.copy(self.prev, 0, 2, self.plus).wait_send()
        self.copy(self.next, 1, 3, self.minus).wait_send()


def kernel(
    q_hbm, kv_hbm, x_hbm, w_hbm, ids_hbm, home_hbm, counts_hbm, renewed_hbm, out_hbm,
    ids, home, counts, renewed, q, w_raw, packed, table, bias, x_own, x_all, w_all, k_near, v_near, k_send, v_send, k_all, v_all,
    mixed, top, total, projected, squares, part_send, part_recv, norm_send, norm_recv, fresh, result,
    local_sem, out_sem, kv1_send, kv1_recv, kv2_send, kv2_recv,
    own_send, own_recv, other_send, other_recv, side_send, side_recv, flow_send, flow_recv,
    lend_send, lend_recv, core_send, core_recv, sum_send, sum_recv,
):
    store, head = lax.axis_index("store"), lax.axis_index("head")
    x, y, z, core = store // 4, store % 4, head // 2, head % 2

    def at_xy(dx, dy):
        return {"store": ((x + dx) % 4) * 4 + (y + dy) % 4, "head": head}

    def at_z(dz):
        return {"store": store, "head": ((z + dz) % 8) * 2 + core}

    sibling = {"store": store, "head": z * 2 + (1 - core)}

    half_of, odd = y // 2, y % 2
    source = z % 2 == half_of
    relay = z % 2 != half_of
    ally = {"store": x * 4 + y + 1 - 2 * odd, "head": head}
    partner = {"store": x * 4 + 3 - y, "head": head}
    x_mine = (z // 2) * 2 + core
    w_mine = x * 2 + odd

    loads = [
        pltpu.make_async_copy(kv_hbm.at[:, 0], k_near.at[x], local_sem.at[0]),
        pltpu.make_async_copy(kv_hbm.at[:, 1], v_near.at[y], local_sem.at[1]),
        pltpu.make_async_copy(w_hbm, w_raw, local_sem.at[3]),
        pltpu.make_async_copy(q_hbm, q, local_sem.at[4]),
        pltpu.make_async_copy(ids_hbm, ids, local_sem.at[5]),
        pltpu.make_async_copy(home_hbm, home, local_sem.at[6]),
        pltpu.make_async_copy(counts_hbm, counts, local_sem.at[7]),
        pltpu.make_async_copy(renewed_hbm, renewed, local_sem.at[8]),
    ]
    for load in loads:
        load.start()
    x_load = pltpu.make_async_copy(x_hbm, x_all.at[x_mine, pl.ds(0, ROWS)], local_sem.at[2])
    x_lent = pltpu.make_async_copy(x_hbm, x_own, local_sem.at[2])
    pl.when(source)(x_load.start)
    pl.when(relay)(x_lent.start)

    barrier = pltpu.get_barrier_semaphore()
    peers = [at_xy(d, 0) for d in (1, 3, 2)] + [at_xy(0, d) for d in (1, 3, 2)]
    peers += [at_z(1), at_z(7), sibling]
    for peer in peers:
        pl.semaphore_signal(barrier, inc=1, device_id=peer, device_id_type=MESH)
    pl.semaphore_wait(barrier, len(peers))

    def sems(ref, *lead):
        return lambda k: ref.at[(*lead, k)]

    def near_at(buf):
        return lambda i, part: buf.at[i] if part is None else buf.at[i, pl.ds(4 * part, 4)]

    def w_at(side, first, rows):
        def at(i, part):
            if part is None:
                return w_all.at[i * 2 + side, pl.ds(first, rows)]
            return w_all.at[i * 2 + side, pl.ds(first + part * (rows // 2), rows // 2)]

        return at

    along_x = (x, at_xy(1, 0), at_xy(3, 0))
    along_y = (y, at_xy(0, 1), at_xy(0, 3))
    k1 = Ring4(near_at(k_near), *along_x, sems(kv1_send, 0), sems(kv1_recv, 0))
    v1 = Ring4(near_at(v_near), *along_y, sems(kv1_send, 1), sems(kv1_recv, 1))
    own = Ring4(w_at(odd, 0, DEEP), *along_x, sems(own_send), sems(own_recv))
    other = Ring4(w_at(1 - odd, 0, DEEP // 2), *along_x, sems(other_send), sems(other_recv))

    def offset(j):
        return j + j // 2 - 2 * (j // 3)

    def side(j, sent=True):
        block = (x + offset(j % 4)) % 4 * 2 + (odd if sent else 1 - odd)
        piece = w_all.at[block, pl.ds(0 if j == 4 else DEEP // 2, DEEP // 2)]
        return remote(piece, piece, side_send.at[j], side_recv.at[j], ally)

    def x_piece(way, dist, w):
        at = (z + (8 - dist if way == 0 else dist)) % 8
        return x_all.at[(at // 2) * 2 + core, pl.ds(256 * w, 256)]

    def flow(way, stage, dist, w):
        piece = x_piece(way, dist, w)
        device = at_z(1 if way == 0 else 7)
        return remote(piece, piece, flow_send.at[way, stage, w], flow_recv.at[way, stage, w], device)

    def lend(half):
        return remote(
            x_own.at[pl.ds(256 * half, 256)], x_all.at[x_mine, pl.ds(ROWS + 256 * half, 256)],
            lend_send.at[half], lend_recv.at[half], partner,
        )

    def to_core(dist, *pieces):
        at = (z + 8 + dist) % 8
        for w in pieces:
            piece = x_all.at[(at // 2) * 2 + core, pl.ds(256 * w, 256)]
            remote(piece, piece, core_send.at[at // 2, w], core_recv.at[at // 2, w], sibling).start()

    def x_start():
        @pl.when(source)
        def _():
            x_load.wait()
            for w in (0, 1):
                flow(0, 0, 0, w).start()
                flow(1, 0, 0, w).start()
            to_core(0, 0, 1)

        @pl.when(relay)
        def _():
            x_lent.wait()
            lend(0).start()
            lend(1).start()

    def x_one():
        @pl.when(relay)
        def _():
            for w in (0, 1):
                for way in (0, 1):
                    flow(way, 0, 1, w).wait_recv()
                    flow(way, 0, 1, w).start()
            to_core(-1, 0, 1)
            to_core(1, 0, 1)

        @pl.when(source)
        def _():
            for w in (2, 3):
                lend(w - 2).wait_recv()
                flow(0, 0, 0, w).start()
                flow(1, 0, 0, w).start()
            to_core(0, 2, 3)

    def x_two(half):
        w = 2 + half

        @pl.when(relay)
        def _():
            for way in (0, 1):
                flow(way, 0, 1, w).wait_recv()
                flow(way, 0, 1, w).start()
            if half:
                to_core(-1, 2, 3)
                to_core(1, 2, 3)

        @pl.when(source)
        def _():
            for way in (0, 1):
                flow(way, 0, 2, half).wait_recv()
            if half:
                to_core(-2, 0, 1)
                to_core(2, 0, 1)

    def x_three(half):
        w = 2 + half

        @pl.when(source)
        def _():
            for way in (0, 1):
                flow(way, 0, 2, w).wait_recv()
                flow(way, 1, 2, w).start()
            if half:
                for way in (0, 1):
                    flow(way, 1, 2, 0).start()
                    flow(way, 1, 2, 1).start()
                to_core(-2, 2, 3)
                to_core(2, 2, 3)

    def x_relayed(part):
        @pl.when(relay)
        def _():
            for half in (0, 1):
                w = 2 * part + half
                for way in (0, 1):
                    flow(way, 1, 3, w).wait_recv()
                    if way == half:
                        flow(way, 1, 3, w).start()
                to_core(-3, w)
                to_core(3, w)

    def x_ended(w):
        @pl.when(source)
        def _():
            flow(w % 2, 1, 4, w).wait_recv()
            to_core(4, w)

    def x_others(w):
        for at in range(4):
            piece = x_all.at[at * 2 + 1 - core, pl.ds(256 * w, 256)]
            remote(piece, piece, core_send.at[at, w], core_recv.at[at, w], sibling).wait_recv()

    def x_drain():
        @pl.when(source)
        def _():
            for way in (0, 1):
                for w in range(4):
                    flow(way, 0, 0, w).wait_send()
                    flow(way, 1, 2, w).wait_send()

        @pl.when(relay)
        def _():
            lend(0).wait_send()
            lend(1).wait_send()
            for way in (0, 1):
                for w in range(4):
                    flow(way, 0, 1, w).wait_send()
                for part in (0, 1):
                    flow(way, 1, 3, 2 * part + way).wait_send()

        for at in range(4):
            for w in range(4):
                piece = x_all.at[at * 2 + core, pl.ds(256 * w, 256)]
                remote(piece, piece, core_send.at[at, w], core_recv.at[at, w], sibling).wait_send()

    def swap(half):
        rows = pl.ds(256 * half, 256)
        return remote(
            part_send.at[rows], part_recv.at[rows], sum_send.at[half], sum_recv.at[half], partner
        )

    swap_norm = remote(norm_send, norm_recv, sum_send.at[2], sum_recv.at[2], partner)

    def k2(r, d):
        return remote(
            k_send.at[(y + d) % 4, r], k_all.at[r, y],
            kv2_send.at[0, r, d - 1], kv2_recv.at[0, r, d - 1], at_xy(0, d),
        )

    def k2_arrived(r, d):
        remote(
            k_send.at[0, r], k_all.at[r, (y + 4 - d) % 4],
            kv2_send.at[0, r, d - 1], kv2_recv.at[0, r, d - 1], at_xy(0, d),
        ).wait_recv()

    def v2(r, d):
        return remote(
            v_send.at[(x + d) % 4, r], v_all.at[r, :, x],
            kv2_send.at[1, r, d - 1], kv2_recv.at[1, r, d - 1], at_xy(d, 0),
        )

    def v2_arrived(r, d):
        remote(
            v_send.at[0, r], v_all.at[r, :, (x + 4 - d) % 4],
            kv2_send.at[1, r, d - 1], kv2_recv.at[1, r, d - 1], at_xy(d, 0),
        ).wait_recv()

    def name_rows():
        named = ids[...]
        stored = lax.fori_loop(
            0, 128, lambda p, rows: jnp.where(named == p, home[p], rows), named, unroll=8
        )
        device = lax.broadcasted_iota(jnp.int32, (SLOTS, 64), 0)
        filled = jnp.zeros((SLOTS, 64), jnp.int32)
        for j in range(SLOTS):
            row = stored[j : j + 1, :]
            filled = jnp.where(device == (row >> 3), j * 8 + (row & 7), filled)
        packed[...] = jnp.zeros_like(packed)
        packed[:, pl.ds(0, 64)] = filled
        move = pltpu.make_async_copy(packed, table, local_sem.at[9])
        move.start()
        move.wait()

    def mask_positions():
        lane = lax.broadcasted_iota(jnp.int32, (1, SPAN), 1)
        block, inner = lane >> 6, lane & 63
        for r in range(REQS):
            mine = store * REQS + r
            place = jnp.zeros((1, SPAN), jnp.int32)
            for b in range(SLOTS):
                slot = table[(b % 4) * 4 + b // 4, mine] // 8
                place = jnp.where(block == b, slot * BLK, place)
            place = place + inner
            shift = jnp.where(place < counts[mine] * BLK, 0.0, MASKED)
            bias[r] = lax.fori_loop(
                0, SEL, lambda i, kept: jnp.where(place == renewed[r, i], MASKED, kept), shift, unroll=8
            )

    def send_keys(first, count):
        @pl.loop(first, first + count)
        def _(r):
            for yd in range(4):
                for xs in range(4):
                    row = table[xs * 4 + y, (x * 4 + yd) * REQS + r] % 8
                    k_send[yd, r, xs] = k_near[xs, row]
            k_all[r, y] = k_send[y, r]
            for d in (1, 3, 2):
                k2(r, d).start()

    def send_values(first, count):
        @pl.loop(first, first + count)
        def _(r):
            for xd in range(4):
                for ys in range(4):
                    row = table[x * 4 + ys, (xd * 4 + y) * REQS + r] % 8
                    v_send[xd, r, ys] = v_near[ys, row]
            for ys in range(4):
                v_all[r, ys, x] = v_send[x, r, ys]
            for d in (1, 3, 2):
                v2(r, d).start()

    def attend_cached(r):
        for d in (1, 3, 2):
            k2_arrived(r, d)
            v2_arrived(r, d)

        @pl.loop(0, QLEN // QTILE)
        def _(t):
            first = pl.multiple_of(t * QTILE, QTILE)
            shift = bias[r]
            for h in (0, 1):
                lanes = pl.ds(h * HD, HD)
                keys = k_all[r, :, :, :, lanes].reshape(SPAN, HD)
                values = v_all[r, :, :, :, lanes].reshape(SPAN, HD)
                scores = dot(q[r, pl.ds(first, QTILE), lanes], keys, NT) * TO_BASE_TWO + shift
                largest = jnp.max(scores, axis=-1, keepdims=True)
                exps = jnp.exp2(scores - largest)
                summed = jnp.sum(exps, axis=-1, keepdims=True)
                mixed[r, pl.ds(first, QTILE), lanes] = dot(exps.astype(jnp.bfloat16), values, NN)
                top[r, pl.ds(first, QTILE), lanes] = jnp.broadcast_to(largest, (QTILE, HD))
                total[r, pl.ds(first, QTILE), lanes] = jnp.broadcast_to(summed, (QTILE, HD))

    def project(part, half):
        rows = pl.ds(ROWS * part + 256 * half, 256)
        summed = dot(x_all[0, rows, :], w_all[0], NN)
        for b in range(1, 8):
            summed = summed + dot(x_all[b, rows, :], w_all[b], NN)
        return summed

    def sum_squares(part):
        squares[...] = jnp.zeros_like(squares)

        @pl.loop(0, 8)
        def _(b):
            wide = x_all[b, pl.ds(ROWS * part, ROWS), :].astype(jnp.float32)
            wide = wide * wide
            squares[...] += (wide[:, 0:128] + wide[:, 128:256]) + (wide[:, 256:384] + wide[:, 384:512])

    x_start()
    loads[0].wait()
    k1.start()
    loads[1].wait()
    v1.start()
    loads[2].wait()
    w_all[w_mine, :, pl.ds(0, FEAT)] = w_raw[:, 0, :]
    w_all[w_mine, :, pl.ds(FEAT, FEAT)] = w_raw[:, 1, :]
    side(4).start()
    loads[4].wait()
    loads[5].wait()
    name_rows()
    k1.forward()
    own.start()
    side(0).start()
    k1.finish()
    send_keys(0, 1)
    x_one()
    v1.forward()
    side(4, False).wait_recv()
    other.start()
    x_two(0)
    own.forward()
    side(1).start()
    side(2).start()
    x_two(1)
    v1.finish()
    send_values(0, 1)
    x_three(0)
    loads[3].wait()
    loads[6].wait()
    loads[7].wait()
    mask_positions()
    other.forward()
    x_three(1)
    own.finish()
    side(3).start()
    send_keys(1, 3)
    send_values(1, 3)
    x_relayed(1)
    attend_cached(0)
    x_ended(2)
    other.finish()
    for j in range(4):
        side(j, False).wait_recv()
    x_others(2)
    part_send[pl.ds(0, 256), :] = project(1, 0).astype(jnp.bfloat16)
    swap(0).start()
    x_ended(3)
    x_others(3)
    part_send[pl.ds(256, 256), :] = project(1, 1).astype(jnp.bfloat16)
    swap(1).start()
    x_relayed(0)
    sum_squares(1)
    turned = jnp.transpose(squares[...])
    norm_send[...] = jnp.broadcast_to(jnp.sum(turned, axis=0, keepdims=True), norm_send.shape)
    swap_norm.start()
    attend_cached(1)
    x_ended(0)
    x_ended(1)
    x_others(0)
    x_others(1)
    sum_squares(0)
    for half in (0, 1):
        projected[pl.ds(256 * half, 256), :] = project(0, half)

    for half in (0, 1):
        swap(half).wait_recv()
    swap_norm.wait_recv()
    lent = jnp.transpose(jnp.broadcast_to(norm_recv[0:1, :], (HD, ROWS)))
    mean = (jnp.sum(squares[...], axis=-1, keepdims=True) + lent) * (1.0 / D)
    scale = lax.rsqrt(mean + EPS)
    for i in range(4):
        lanes = pl.ds(i * HD, HD)
        summed = projected[:, lanes] + part_recv[:, lanes].astype(jnp.float32)
        at = i * HD if i < 2 else FEAT + (i - 2) * 2 * HD
        fresh[:, pl.ds(at, HD)] = (summed * scale).astype(jnp.bfloat16)
        if i >= 2:
            fresh[:, pl.ds(at + HD, HD)] = jnp.ones((ROWS, HD), jnp.bfloat16)

    def store_result(r):
        return pltpu.make_async_copy(result.at[r], out_hbm.at[r], out_sem.at[r])

    @pl.loop(0, 2)
    def _(r):
        rows = pl.ds(pl.multiple_of(r * SEL, SEL), SEL)
        for h in (0, 1):
            lanes = pl.ds(h * HD, HD)
            scores = dot(q[r, :, lanes], fresh[rows, lanes], NT) * TO_BASE_TWO
            before = top[r, :, lanes]
            largest = jnp.maximum(before, jnp.max(scores, axis=-1, keepdims=True))
            exps = jnp.exp2(scores - largest)
            fade = jnp.exp2(before - largest)
            both = dot(exps.astype(jnp.bfloat16), fresh[rows, pl.ds(FEAT + h * 2 * HD, 2 * HD)], NN)
            attended = (mixed[r, :, lanes] * fade + both[:, 0:HD]) / (total[r, :, lanes] * fade + both[:, HD:])
            result[r, :, lanes] = attended.astype(jnp.bfloat16)
        store_result(r).start()

    @pl.loop(2, REQS)
    def _(r):
        for d in (1, 3, 2):
            k2_arrived(r, d)
            v2_arrived(r, d)

        @pl.loop(0, QLEN // QTILE)
        def _(t):
            rows = pl.ds(pl.multiple_of(t * QTILE, QTILE), QTILE)
            shift = bias[r]
            for h in (0, 1):
                lanes = pl.ds(h * HD, HD)
                tail = pl.ds(pl.multiple_of(r * SEL, SEL), SEL)
                keys = k_all[r, :, :, :, lanes].reshape(SPAN, HD)
                values = v_all[r, :, :, :, lanes].reshape(SPAN, HD)
                scores = dot(q[r, rows, lanes], keys, NT) * TO_BASE_TWO + shift
                extra = dot(q[r, rows, lanes], fresh[tail, lanes], NT) * TO_BASE_TWO
                largest = jnp.maximum(
                    jnp.max(scores, axis=-1, keepdims=True), jnp.max(extra, axis=-1, keepdims=True)
                )
                exps = jnp.exp2(scores - largest)
                more = jnp.exp2(extra - largest)
                summed = jnp.sum(exps, axis=-1, keepdims=True) + jnp.sum(more, axis=-1, keepdims=True)
                blend = dot(exps.astype(jnp.bfloat16), values, NN) + dot(
                    more.astype(jnp.bfloat16), fresh[tail, pl.ds(FEAT + h * 2 * HD, HD)], NN
                )
                result[r, rows, lanes] = (blend / summed).astype(jnp.bfloat16)

        store_result(r).start()

    for ring in (k1, v1, own, other):
        ring.drain()
    for j in range(5):
        side(j).wait_send()

    @pl.loop(0, REQS)
    def _(r):
        for d in (1, 2, 3):
            k2(r, d).wait_send()
            v2(r, d).wait_send()

    x_drain()
    swap(0).wait_send()
    swap(1).wait_send()
    swap_norm.wait_send()
    for r in range(REQS):
        store_result(r).wait()


def attend(q, kv, rows, weights, ids, home, counts, renewed):
    hbm = pl.BlockSpec(memory_space=pltpu.HBM)
    bf, f32 = jnp.bfloat16, jnp.float32
    dma = pltpu.SemaphoreType.DMA
    return pl.pallas_call(
        kernel,
        out_shape=jax.ShapeDtypeStruct((REQS, QLEN, FEAT), bf),
        in_specs=[hbm] * 8,
        out_specs=pl.BlockSpec(memory_space=pl.ANY),
        scratch_shapes=[
            pltpu.VMEM((SLOTS, 64), jnp.int32),
            pltpu.SMEM((128,), jnp.int32),
            pltpu.SMEM((64,), jnp.int32),
            pltpu.SMEM((REQS, SEL), jnp.int32),
            pltpu.VMEM((REQS, QLEN, FEAT), bf),
            pltpu.VMEM((DEEP, 2, FEAT), bf),
            pltpu.VMEM((SLOTS, 128), jnp.int32),
            pltpu.SMEM((SLOTS, 128), jnp.int32),
            pltpu.VMEM((REQS, 1, SPAN), f32),
            pltpu.VMEM((ROWS, DEEP), bf),
            pltpu.VMEM((8, 2 * ROWS, DEEP), bf),
            pltpu.VMEM((8, DEEP, 2 * FEAT), bf),
            pltpu.VMEM((4, 8, BLK, FEAT), bf),
            pltpu.VMEM((4, 8, BLK, FEAT), bf),
            pltpu.VMEM((4, REQS, 4, BLK, FEAT), bf),
            pltpu.VMEM((4, REQS, 4, BLK, FEAT), bf),
            pltpu.VMEM((REQS, 4, 4, BLK, FEAT), bf),
            pltpu.VMEM((REQS, 4, 4, BLK, FEAT), bf),
            pltpu.VMEM((REQS, QLEN, FEAT), f32),
            pltpu.VMEM((REQS, QLEN, FEAT), f32),
            pltpu.VMEM((REQS, QLEN, FEAT), f32),
            pltpu.VMEM((ROWS, 2 * FEAT), f32),
            pltpu.VMEM((ROWS, HD), f32),
            pltpu.VMEM((ROWS, 2 * FEAT), bf),
            pltpu.VMEM((ROWS, 2 * FEAT), bf),
            pltpu.VMEM((8, ROWS), f32),
            pltpu.VMEM((8, ROWS), f32),
            pltpu.VMEM((ROWS, 3 * FEAT), bf),
            pltpu.VMEM((REQS, QLEN, FEAT), bf),
            dma((11,)),
            dma((REQS,)),
            dma((2, 4)), dma((2, 4)),
            dma((2, REQS, 3)), dma((2, REQS, 3)),
            dma((4,)), dma((4,)),
            dma((4,)), dma((4,)),
            dma((5,)), dma((5,)),
            dma((2, 2, 4)), dma((2, 2, 4)),
            dma((2,)), dma((2,)),
            dma((4, 4)), dma((4, 4)),
            dma((3,)), dma((3,)),
        ],
        compiler_params=pltpu.CompilerParams(
            collective_id=0, has_side_effects=True, vmem_limit_bytes=60 * 1024 * 1024
        ),
        cost_estimate=pl.CostEstimate(
            flops=14_000_000_000, bytes_accessed=8_000_000, transcendentals=10_000_000
        ),
        name="blend",
    )(q, kv, rows, weights, ids, home, counts, renewed)


def local(
    queries, kv_store, hidden_rows, w_kv, passage_ids, passage_home, passage_counts, recompute_pos
):
    return attend(
        queries,
        kv_store,
        hidden_rows.reshape(ROWS, DEEP),
        w_kv,
        passage_ids.T,
        passage_home,
        passage_counts,
        recompute_pos,
    )


def solution(mesh):
    placed = (
        P("store", None, "head"),
        P("store", None, None, "head"),
        P("store", None, "head"),
        P("store", None, "head"),
        P(),
        P(),
        P(),
        P("store", None),
    )
    return jax.shard_map(
        local, mesh=mesh, in_specs=placed, out_specs=P("store", None, "head"), check_vma=False
    )
```
